32 devices in a mesh: expert: 4 (over z), mp: 8 (over y, x, core).
Axes of the slice: x: 2, y: 2, z: 4, core: 2. Of those that a mesh axis runs over, the one named last changes fastest.
Arguments:
- x_tokens: bfloat16 [512, 2048], P('expert', 'mp'), may hold values from -6 to 6
- cotangent: bfloat16 [512, 2048], P('expert', 'mp'), may hold values from -2 to 2
- w_gate: bfloat16 [4, 1024, 8192], P('expert', None, 'mp'), may hold values from -0.125 to 0.125
- w_up: bfloat16 [4, 1024, 8192], P('expert', None, 'mp'), may hold values from -0.125 to 0.125
- w_down: bfloat16 [4, 8192, 1024], P('expert', 'mp'), may hold values from -0.125 to 0.125
- combine: float32 [8, 128], P('expert'), may hold values from 0.1 to 1
- indices: int32 [8, 128], replicated, may hold values from -1 to 511, as said below
Outputs:
- grad_tokens: bfloat16 [512, 2048], P('expert', 'mp')
- grad_gate: bfloat16 [4, 1024, 8192], P('expert', None, 'mp')
- grad_up: bfloat16 [4, 1024, 8192], P('expert', None, 'mp')
- grad_down: bfloat16 [4, 8192, 1024], P('expert', 'mp')
- grad_combine: float32 [8, 128], P('expert')
The draws below stay inside these ranges and needn't reach their ends.
Inputs may be any that keep to these rules, and one draw needn't show every extreme that they name: `indices`: each row lists the tokens one expert chose, in increasing order, then -1 in its remaining slots. Tokens are owned in blocks of 128 along expert; one expert takes at most 64 tokens from one block, and in every row some block gives exactly 64. In every draw some expert fills all 128 slots.
All inputs are finite; a program needn't handle non-finite values.
Results may differ from the reference program's by a relative error of at most 0.022.
Values may be sent and summed in bfloat16 or wider, within the bound.
A program may use at most 64 MiB of HBM per device.

```python
import jax
import jax.numpy as jnp
from jax import lax

D = 2048
FF = 2048
EXP_DEV = 2
TOK_DEV = 128
GROUPS = 4
EXPERTS = 8
TOKENS = 512
CAP = 128
PEER = 64
N_EXPERT = 4
N_MP = 8


def draw_indices(key, part):
    key = jax.random.fold_in(key, 7)
    keys = jax.random.split(key, 6)
    pairs = N_EXPERT // 2
    first_count = jax.random.randint(keys[0], (EXPERTS, pairs), PEER // 4, PEER + 1)
    remaining = PEER - first_count
    second_count = jax.random.randint(keys[1], (EXPERTS, pairs), remaining // 2, remaining + 1)
    forced_pair = jax.random.randint(keys[2], (EXPERTS, 1), 0, pairs)
    pair_ids = jnp.arange(pairs, dtype=jnp.int32)[None, :]
    first_count = jnp.where(pair_ids == forced_pair, PEER, first_count)
    full_expert = jax.random.randint(keys[3], (), 0, EXPERTS)
    expert_ids = jnp.arange(EXPERTS, dtype=jnp.int32)[:, None]
    second_count = jnp.where(expert_ids == full_expert, PEER - first_count, second_count)
    second_count = jnp.where(pair_ids == forced_pair, 0, second_count)
    paired = jnp.concatenate([first_count, second_count], axis=1)
    orders = jax.vmap(lambda item: jax.random.permutation(item, N_EXPERT))(jax.random.split(keys[4], EXPERTS))
    counts = jnp.take_along_axis(paired, orders, axis=1)
    ranks = jax.vmap(lambda item: jax.random.permutation(item, TOK_DEV))(jax.random.split(keys[5], EXPERTS * N_EXPERT))
    ranks = ranks.reshape(EXPERTS, N_EXPERT, TOK_DEV)
    picked = (ranks < counts[:, :, None]).reshape(EXPERTS, TOKENS)
    position = jnp.cumsum(picked.astype(jnp.int32), axis=1) - 1
    position = jnp.where(picked, position, CAP)
    token_ids = jnp.broadcast_to(jnp.arange(TOKENS, dtype=jnp.int32)[None, :], (EXPERTS, TOKENS))
    row_ids = jnp.broadcast_to(jnp.arange(EXPERTS, dtype=jnp.int32)[:, None], (EXPERTS, TOKENS))
    table = jnp.full((EXPERTS, CAP + 1), -1, jnp.int32).at[row_ids, position].set(token_ids)
    return table[:, :CAP]


def steps_of(own_key, extent, cuts, least, top_value):
    loudness = 1.0
    for dim, blocks in cuts:
        draws = jax.random.uniform(jax.random.fold_in(jax.random.fold_in(own_key, 6), dim), (blocks,), jnp.float32, least / len(cuts), top_value / len(cuts))
        loudness = loudness * jnp.repeat(jnp.exp(draws), extent[dim] // blocks).reshape((-1,) + (1,) * (len(extent) - 1 - dim))
    return loudness


def noise(own_key, extent, scale, bound, cuts=(), kind=jnp.bfloat16):
    entries = scale * jax.random.normal(own_key, extent, jnp.float32)
    if cuts:
        entries = entries * steps_of(own_key, extent, cuts, -0.22, 0.18)
    return jnp.clip(entries, -bound, bound).astype(kind)


def setup_inputs(seed: int = 0) -> dict:
    arg_keys = jax.random.split(jax.random.key(seed), 8)
    return {
        "x_tokens": noise(arg_keys[0], (TOKENS, D), 1.0, 6.0, ((0, 4), (1, 8))),
        "cotangent": noise(arg_keys[1], (TOKENS, D), 0.3, 2.0, ((0, 4), (1, 8))),
        "w_gate": noise(arg_keys[2], (GROUPS, D // 2, 2 * EXP_DEV * FF), D ** -0.5, 0.125, ((0, 4), (2, 8))),
        "w_up": noise(arg_keys[3], (GROUPS, D // 2, 2 * EXP_DEV * FF), D ** -0.5, 0.125, ((0, 4), (2, 8))),
        "w_down": noise(arg_keys[4], (GROUPS, 2 * EXP_DEV * FF, D // 2), FF ** -0.5, 0.125, ((0, 4), (1, 8))),
        "combine": jnp.clip(0.1 + 0.9 * jax.random.uniform(arg_keys[5], (EXPERTS, CAP), jnp.float32) ** steps_of(arg_keys[5], (EXPERTS, CAP), ((0, 4),), -0.2, 0.2), 0.1, 1.0),
        "indices": draw_indices(jax.random.fold_in(arg_keys[7], 71), 0),
    }


def expert_grads(rows_in, rows_out, wg, wu, wd, slot_weight):
    gate_pre = jnp.dot(rows_in, wg, preferred_element_type=jnp.float32)
    up_pre = jnp.dot(rows_in, wu, preferred_element_type=jnp.float32)
    sigmoid_gate = jax.nn.sigmoid(gate_pre)
    activation = (gate_pre * sigmoid_gate * up_pre).astype(jnp.bfloat16)
    back_grad = lax.dot_general(rows_out, wd, (((1,), (1,)), ((), ())), preferred_element_type=jnp.float32)
    slot_term = jnp.sum(activation.astype(jnp.float32) * back_grad, axis=1)
    scaled_out = (slot_weight[:, None] * rows_out.astype(jnp.float32)).astype(jnp.bfloat16)
    grad_down = lax.dot_general(activation, scaled_out, (((0,), (0,)), ((), ())), preferred_element_type=jnp.float32).astype(jnp.bfloat16)
    d_act = slot_weight[:, None] * back_grad
    d_gate = (d_act * up_pre * sigmoid_gate * (1.0 + gate_pre * (1.0 - sigmoid_gate))).astype(jnp.bfloat16)
    d_up = (d_act * gate_pre * sigmoid_gate).astype(jnp.bfloat16)
    grad_gate = lax.dot_general(rows_in, d_gate, (((0,), (0,)), ((), ())), preferred_element_type=jnp.float32).astype(jnp.bfloat16)
    grad_up = lax.dot_general(rows_in, d_up, (((0,), (0,)), ((), ())), preferred_element_type=jnp.float32).astype(jnp.bfloat16)
    blocks = N_MP // (2 * EXP_DEV)
    block_width = FF // blocks
    pieces = jnp.einsum("cbh,dbh->bcd", d_gate.astype(jnp.float32).reshape(CAP, blocks, block_width),
                        wg.astype(jnp.float32).reshape(D, blocks, block_width), precision=lax.Precision.HIGHEST)
    pieces = pieces + jnp.einsum("cbh,dbh->bcd", d_up.astype(jnp.float32).reshape(CAP, blocks, block_width),
                                 wu.astype(jnp.float32).reshape(D, blocks, block_width), precision=lax.Precision.HIGHEST)
    rounded = lax.optimization_barrier(pieces.astype(jnp.bfloat16))
    contrib = jnp.sum(rounded.astype(jnp.float32), axis=0)
    return slot_term, grad_gate, grad_up, grad_down, contrib


def unpack_in(group_weight, member):
    part = group_weight.reshape(D // 2, EXP_DEV, 2, FF)[:, member]
    return jnp.transpose(part, (1, 0, 2)).reshape(D, FF)


def pack_in(mats):
    stacked = jnp.stack(mats).reshape(EXP_DEV, 2, D // 2, FF)
    return jnp.transpose(stacked, (2, 0, 1, 3)).reshape(D // 2, 2 * EXP_DEV * FF)


def unpack_down(group_weight, member):
    part = group_weight.reshape(EXP_DEV, 2, FF, D // 2)[member]
    return jnp.transpose(part, (1, 0, 2)).reshape(FF, D)


def pack_down(mats):
    stacked = jnp.stack(mats).reshape(EXP_DEV, FF, 2, D // 2)
    return jnp.transpose(stacked, (0, 2, 1, 3)).reshape(2 * EXP_DEV * FF, D // 2)


def reference(x_tokens, cotangent, w_gate, w_up, w_down, combine, indices):
    def one_group(group_index):
        wg_group = lax.dynamic_index_in_dim(w_gate, group_index, 0, keepdims=False)
        wu_group = lax.dynamic_index_in_dim(w_up, group_index, 0, keepdims=False)
        wd_group = lax.dynamic_index_in_dim(w_down, group_index, 0, keepdims=False)
        terms, gates, ups, downs, contribs = [], [], [], [], []
        for member in range(EXP_DEV):
            expert_id = group_index * EXP_DEV + member
            chosen = lax.dynamic_index_in_dim(indices, expert_id, 0, keepdims=False)
            slot_weight = lax.dynamic_index_in_dim(combine, expert_id, 0, keepdims=False)
            slot_valid = chosen >= 0
            safe = jnp.where(slot_valid, chosen, 0).astype(jnp.int32)
            rows_in = jnp.where(slot_valid[:, None], x_tokens[safe], jnp.zeros((), jnp.bfloat16))
            rows_out = jnp.where(slot_valid[:, None], cotangent[safe], jnp.zeros((), jnp.bfloat16))
            wg = unpack_in(wg_group, member)
            wu = unpack_in(wu_group, member)
            wd = unpack_down(wd_group, member)
            result = expert_grads(rows_in, rows_out, wg, wu, wd, slot_weight)
            terms.append(result[0])
            gates.append(result[1])
            ups.append(result[2])
            downs.append(result[3])
            contribs.append(result[4])
        return (jnp.stack(terms), pack_in(gates), pack_in(ups), pack_down(downs), jnp.stack(contribs))

    terms, grad_gate, grad_up, grad_down, contribs = lax.map(one_group, jnp.arange(N_EXPERT, dtype=jnp.int32))
    grad_combine = terms.reshape(EXPERTS, CAP)
    targets = jnp.where(indices >= 0, indices, TOKENS).astype(jnp.int32).reshape(-1)
    summed = jnp.zeros((TOKENS + 1, D), jnp.float32).at[targets].add(contribs.reshape(-1, D))
    grad_tokens = summed[:TOKENS].astype(jnp.bfloat16)
    return grad_tokens, grad_gate, grad_up, grad_down, grad_combine
```

```python
import functools

import jax
import jax.numpy as jnp
from jax import lax
from jax.experimental import pallas as pl
from jax.experimental.pallas import tpu as pltpu
from jax.sharding import PartitionSpec as P

MESH = pl.DeviceIdType.MESH
F32 = jnp.float32
BF16 = jnp.bfloat16


def nn(a, b):
    return jnp.dot(a, b, preferred_element_type=F32)


def nt(a, b):
    return lax.dot_general(a, b, (((1,), (1,)), ((), ())), preferred_element_type=F32)


def tn(a, b):
    return lax.dot_general(a, b, (((0,), (0,)), ((), ())), preferred_element_type=F32)


def layer_kernel(
    dims,
    x_ref, cot_ref, wg_hbm, wu_hbm, wd_hbm, combine_ref, idx_ref,
    tokens_ref, terms_ref, rows_in_ref, scaled_ref, act_ref, dgate_ref, dup_ref,
    wg, wu, wd, tok, gathered, rx, rows_out, mine, ex_send, ex_recv,
    term_buf, red_send, red_recv, back_send, back_recv, ret_send, ret_recv,
    w_sem, z_send, z_recv, m_send, m_recv, f_send, x_send, x_recv,
    c_send, c_recv, r_send, r_recv, b_send, b_recv, t_send, t_recv,
):
    groups, lanes, exp_dev, blocks, half_lanes, tok_dev, width, capacity, hidden, chunk = dims
    chunks = hidden // chunk
    z = lax.axis_index("expert")
    lane = lax.axis_index("mp")
    own_b = lax.rem(lane, blocks)
    own_h = lax.rem(lax.div(lane, blocks), 2)
    own_e = lax.div(lane, 2 * blocks)
    feat_half = lax.div(lane, half_lanes)
    feat_pos = lax.rem(lane, half_lanes)

    def lane_of(e, h, b):
        return (e * 2 + h) * blocks + b

    def remote(src, dst, ssem, rsem, to_z, to_lane):
        return pltpu.make_async_remote_copy(
            src_ref=src, dst_ref=dst, send_sem=ssem, recv_sem=rsem,
            device_id=(to_z, to_lane), device_id_type=MESH,
        )

    def arrived(ref, ssem, rsem):
        remote(ref, ref, ssem, rsem, z, lane).wait_recv()

    loads = [
        pltpu.make_async_copy(src.at[0], dst, w_sem.at[i])
        for i, (src, dst) in enumerate(((wg_hbm, wg), (wu_hbm, wu), (wd_hbm, wd)))
    ]
    for load in loads:
        load.start()

    barrier = pltpu.get_barrier_semaphore()
    for d in range(1, groups):
        pl.semaphore_signal(barrier, inc=1, device_id=(lax.rem(z + d, groups), lane), device_id_type=MESH)
    for d in range(1, lanes):
        pl.semaphore_signal(barrier, inc=1, device_id=(z, lax.rem(lane + d, lanes)), device_id_type=MESH)
    pl.semaphore_wait(barrier, groups + lanes - 2)

    sends = []
    for kind, src in ((0, x_ref), (1, cot_ref)):
        for d in range(1, groups):
            copy = remote(src, tok.at[kind, z], z_send.at[kind, d], z_recv.at[kind, z],
                          lax.rem(z + d, groups), lane)
            copy.start()
            sends.append(copy)
    tok[0, z] = x_ref[...]
    tok[1, z] = cot_ref[...]

    eye = (
        lax.broadcasted_iota(jnp.int32, (capacity, capacity), 0)
        == lax.broadcasted_iota(jnp.int32, (capacity, capacity), 1)
    )

    def column(row):
        return jnp.sum(jnp.where(eye, jnp.broadcast_to(row, (capacity, capacity)), 0.0), axis=1, keepdims=True)

    idx_rows = [idx_ref[pl.ds(z * exp_dev + e, 1), :] for e in range(exp_dev)]
    idx_cols = [column(row.astype(F32)).astype(jnp.int32) for row in idx_rows]
    weight = column(combine_ref[pl.ds(own_e, 1), :])

    def exchange_rows(kind):
        for d in range(1, groups):
            s = lax.rem(z + d, groups)
            arrived(tok.at[kind, s], z_send.at[kind, d], z_recv.at[kind, s])
        for e in range(exp_dev):
            total = jnp.zeros((capacity, width), F32)
            for g in range(groups):
                ids = lax.broadcasted_iota(jnp.int32, (capacity, tok_dev), 1) + g * tok_dev
                pick = jnp.where(ids == idx_cols[e], 1.0, 0.0).astype(BF16)
                total += nn(pick, tok[kind, g])
            gathered[kind, e] = total.astype(BF16)
            target = lane_of(e, feat_half, own_b)

            @pl.when(target == lane)
            def _():
                rx[kind, feat_pos] = gathered[kind, e]

            @pl.when(target != lane)
            def _():
                remote(gathered.at[kind, e], rx.at[kind, feat_pos], m_send.at[kind, e],
                       m_recv.at[kind, feat_pos], z, target).start()

        for j in range(exp_dev):
            p = j * blocks + own_b
            source = own_h * half_lanes + p

            @pl.when(source != lane)
            def _():
                arrived(rx.at[kind, p], m_send.at[kind, 0], m_recv.at[kind, p])

            for d in range(1, blocks):
                copy = remote(rx.at[kind, p], rx.at[kind, p], f_send.at[kind, j, d], m_recv.at[kind, p],
                              z, lane_of(own_e, own_h, lax.rem(own_b + d, blocks)))
                copy.start()
                sends.append(copy)
        for d in range(1, blocks):
            for j in range(exp_dev):
                p = j * blocks + lax.rem(own_b + d, blocks)
                arrived(rx.at[kind, p], m_send.at[kind, 0], m_recv.at[kind, p])

    partner = lane_of(own_e, 1 - own_h, own_b)

    def exchange_sum(which, c, value):
        cols = slice(c * chunk, (c + 1) * chunk)
        mine[which, :, cols] = value
        ex_send[which, c] = value.astype(BF16)
        copy = remote(ex_send.at[which, c], ex_recv.at[which, c], x_send.at[which, c],
                      x_recv.at[which, c], z, partner)
        copy.start()
        sends.append(copy)

    exchange_rows(0)
    for p in range(half_lanes):
        rows_in_ref[:, p * width:(p + 1) * width] = rx[0, p]
    loads[0].wait()
    loads[1].wait()
    for c in range(chunks):
        cols = slice(c * chunk, (c + 1) * chunk)
        exchange_sum(0, c, nn(rows_in_ref[...], wg[:, cols]))
        exchange_sum(1, c, nn(rows_in_ref[...], wu[:, cols]))

    exchange_rows(1)
    for p in range(half_lanes):
        part = rx[1, p]
        rows_out[:, p * width:(p + 1) * width] = part
        scaled_ref[:, p * width:(p + 1) * width] = (weight * part.astype(F32)).astype(BF16)
    loads[2].wait()
    for c in range(chunks):
        cols = slice(c * chunk, (c + 1) * chunk)
        exchange_sum(2, c, nt(rows_out[...], wd[cols, :]))

    slot_term = jnp.zeros((capacity, 1), F32)
    for c in range(chunks):
        cols = slice(c * chunk, (c + 1) * chunk)
        for which in range(3):
            arrived(ex_recv.at[which, c], x_send.at[which, c], x_recv.at[which, c])
        gate = mine[0, :, cols] + ex_recv[0, c].astype(F32)
        up = mine[1, :, cols] + ex_recv[1, c].astype(F32)
        back = mine[2, :, cols] + ex_recv[2, c].astype(F32)
        s = jax.nn.sigmoid(gate)
        act = (gate * s * up).astype(BF16)
        act_ref[:, cols] = act
        slot_term += jnp.sum(act.astype(F32) * back, axis=1, keepdims=True)
        a = weight * back
        dgate_ref[:, cols] = (a * up * s * (1.0 + gate * (1.0 - s))).astype(BF16)
        dup_ref[:, cols] = (a * gate * s).astype(BF16)

    def block_part(p):
        rows = pl.ds(pl.multiple_of(p * width, width), width)
        return nt(dgate_ref[...], wg[rows, :]) + nt(dup_ref[...], wu[rows, :])

    for d in range(1, blocks):
        to_b = lax.rem(own_b + d, blocks)
        for j in range(exp_dev):
            red_send[d, j] = block_part(j * blocks + to_b).astype(BF16)
            copy = remote(red_send.at[d, j], red_recv.at[own_b, j], r_send.at[d, j], r_recv.at[own_b, j],
                          z, lane_of(own_e, own_h, to_b))
            copy.start()
            sends.append(copy)
    for j in range(exp_dev):
        total = block_part(j * blocks + own_b).astype(BF16).astype(F32)
        for d in range(1, blocks):
            from_b = lax.rem(own_b + d, blocks)
            arrived(red_recv.at[from_b, j], r_send.at[d, j], r_recv.at[from_b, j])
            total += red_recv[from_b, j].astype(F32)
        back_send[j] = total.astype(BF16)
        target = own_h * half_lanes + j * blocks + own_b

        @pl.when(target == lane)
        def _():
            back_recv[own_e] = back_send[j]

        @pl.when(target != lane)
        def _():
            remote(back_send.at[j], back_recv.at[own_e], b_send.at[j], b_recv.at[own_e], z, target).start()

    term_row = jnp.sum(jnp.where(eye, jnp.broadcast_to(slot_term, (capacity, capacity)), 0.0), axis=0, keepdims=True)

    @pl.when(own_h == 0)
    def _():
        term_buf[own_e, own_b] = jnp.broadcast_to(term_row, (8, capacity))
        for d in range(1, lanes):
            remote(term_buf.at[own_e, own_b], term_buf.at[own_e, own_b], c_send.at[d],
                   c_recv.at[own_e, own_b], z, lax.rem(lane + d, lanes)).start()

    for e in range(exp_dev):
        source = lane_of(e, feat_half, own_b)

        @pl.when(source != lane)
        def _():
            arrived(back_recv.at[e], b_send.at[0], b_recv.at[e])

    def token_part(g):
        total = jnp.zeros((tok_dev, width), F32)
        for e in range(exp_dev):
            ids = lax.broadcasted_iota(jnp.int32, (tok_dev, capacity), 0) + g * tok_dev
            put = jnp.where(ids == idx_rows[e], 1.0, 0.0).astype(BF16)
            total += nn(put, back_recv[e])
        return total

    for d in range(1, groups):
        g = lax.rem(z + d, groups)
        ret_send[d] = token_part(g).astype(BF16)
        copy = remote(ret_send.at[d], ret_recv.at[z], t_send.at[d], t_recv.at[z], g, lane)
        copy.start()
        sends.append(copy)
    total = token_part(z)

    for e in range(exp_dev):
        for b in range(blocks):
            @pl.when(lane_of(e, 0, b) != lane)
            def _():
                arrived(term_buf.at[e, b], c_send.at[1], c_recv.at[e, b])
        row = term_buf[e, 0, 0:1, :]
        for b in range(1, blocks):
            row += term_buf[e, b, 0:1, :]
        terms_ref[e:e + 1, :] = row

    for d in range(1, groups):
        g = lax.rem(z + d, groups)
        arrived(ret_recv.at[g], t_send.at[d], t_recv.at[g])
        total += ret_recv[g].astype(F32)
    tokens_ref[...] = total.astype(BF16)

    for copy in sends:
        copy.wait_send()
    for e in range(exp_dev):
        target = lane_of(e, feat_half, own_b)

        @pl.when(target != lane)
        def _():
            for kind in range(2):
                remote(gathered.at[kind, e], rx.at[kind, feat_pos], m_send.at[kind, e],
                       m_recv.at[kind, feat_pos], z, target).wait_send()

    for j in range(exp_dev):
        target = own_h * half_lanes + j * blocks + own_b

        @pl.when(target != lane)
        def _():
            remote(back_send.at[j], back_recv.at[own_e], b_send.at[j], b_recv.at[own_e], z, target).wait_send()

    @pl.when(own_h == 0)
    def _():
        for d in range(1, lanes):
            remote(term_buf.at[own_e, own_b], term_buf.at[own_e, own_b], c_send.at[d],
                   c_recv.at[own_e, own_b], z, lax.rem(lane + d, lanes)).wait_send()


def weight_kernel(rows_in, scaled, act, dgate, dup, out_gate, out_up, out_down):
    out_gate[0] = tn(rows_in[...], dgate[...]).astype(BF16)
    out_up[0] = tn(rows_in[...], dup[...]).astype(BF16)
    out_down[0] = tn(act[...], scaled[...]).astype(BF16)


def local(x_tokens, cotangent, w_gate, w_up, w_down, combine, indices):
    groups = lax.axis_size("expert")
    lanes = lax.axis_size("mp")
    tok_dev, width = x_tokens.shape
    experts, capacity = indices.shape
    exp_dev = experts // groups
    blocks = lanes // (2 * exp_dev)
    half_lanes = lanes // 2
    half_width, hidden = w_gate.shape[1:]
    chunk = min(hidden, 256)
    chunks = hidden // chunk
    dims = (groups, lanes, exp_dev, blocks, half_lanes, tok_dev, width, capacity, hidden, chunk)
    vmem = pl.BlockSpec(memory_space=pltpu.VMEM)
    anywhere = pl.BlockSpec(memory_space=pl.ANY)
    dma = pltpu.SemaphoreType.DMA
    slot_half = jax.ShapeDtypeStruct((capacity, half_width), BF16)
    slot_hidden = jax.ShapeDtypeStruct((capacity, hidden), BF16)
    grad_tokens, grad_combine, rows_in, scaled, act, dgate, dup = pl.pallas_call(
        functools.partial(layer_kernel, dims),
        out_shape=[
            jax.ShapeDtypeStruct((tok_dev, width), BF16),
            jax.ShapeDtypeStruct((exp_dev, capacity), F32),
            slot_half, slot_half, slot_hidden, slot_hidden, slot_hidden,
        ],
        in_specs=[vmem, vmem, anywhere, anywhere, anywhere, vmem, vmem],
        out_specs=[vmem] * 7,
        scratch_shapes=[
            pltpu.VMEM((half_width, hidden), BF16),
            pltpu.VMEM((half_width, hidden), BF16),
            pltpu.VMEM((hidden, half_width), BF16),
            pltpu.VMEM((2, groups, tok_dev, width), BF16),
            pltpu.VMEM((2, exp_dev, capacity, width), BF16),
            pltpu.VMEM((2, half_lanes, capacity, width), BF16),
            pltpu.VMEM((capacity, half_width), BF16),
            pltpu.VMEM((3, capacity, hidden), F32),
            pltpu.VMEM((3, chunks, capacity, chunk), BF16),
            pltpu.VMEM((3, chunks, capacity, chunk), BF16),
            pltpu.VMEM((exp_dev, blocks, 8, capacity), F32),
            pltpu.VMEM((blocks, exp_dev, capacity, width), BF16),
            pltpu.VMEM((blocks, exp_dev, capacity, width), BF16),
            pltpu.VMEM((exp_dev, capacity, width), BF16),
            pltpu.VMEM((exp_dev, capacity, width), BF16),
            pltpu.VMEM((groups, tok_dev, width), BF16),
            pltpu.VMEM((groups, tok_dev, width), BF16),
            dma((3,)), dma((2, groups)), dma((2, groups)),
            dma((2, exp_dev)), dma((2, half_lanes)), dma((2, exp_dev, blocks)),
            dma((3, chunks)), dma((3, chunks)),
            dma((lanes,)), dma((exp_dev, blocks)),
            dma((blocks, exp_dev)), dma((blocks, exp_dev)),
            dma((exp_dev,)), dma((exp_dev,)),
            dma((groups,)), dma((groups,)),
        ],
        compiler_params=pltpu.CompilerParams(
            collective_id=0, has_side_effects=True, vmem_limit_bytes=40 * 1024 * 1024
        ),
        name="layer",
    )(x_tokens, cotangent, w_gate, w_up, w_down, combine, indices)

    steps = min(4, hidden // 128)
    rows = half_width // steps
    units = hidden // steps
    grad_gate, grad_up, grad_down = pl.pallas_call(
        weight_kernel,
        grid=(steps,),
        out_shape=[
            jax.ShapeDtypeStruct(w_gate.shape, BF16),
            jax.ShapeDtypeStruct(w_up.shape, BF16),
            jax.ShapeDtypeStruct(w_down.shape, BF16),
        ],
        in_specs=[
            pl.BlockSpec((capacity, rows), lambda i: (0, i)),
            pl.BlockSpec((capacity, half_width), lambda i: (0, 0)),
            pl.BlockSpec((capacity, units), lambda i: (0, i)),
            pl.BlockSpec((capacity, hidden), lambda i: (0, 0)),
            pl.BlockSpec((capacity, hidden), lambda i: (0, 0)),
        ],
        out_specs=[
            pl.BlockSpec((1, rows, hidden), lambda i: (0, i, 0)),
            pl.BlockSpec((1, rows, hidden), lambda i: (0, i, 0)),
            pl.BlockSpec((1, units, half_width), lambda i: (0, i, 0)),
        ],
        compiler_params=pltpu.CompilerParams(vmem_limit_bytes=32 * 1024 * 1024),
        name="weight_grads",
    )(rows_in, scaled, act, dgate, dup)
    return grad_tokens, grad_gate, grad_up, grad_down, grad_combine


def solution(mesh):
    placed = (
        P("expert", "mp"),
        P("expert", "mp"),
        P("expert", None, "mp"),
        P("expert", None, "mp"),
        P("expert", "mp", None),
        P("expert", None),
        P(),
    )
    return jax.shard_map(
        local,
        mesh=mesh,
        in_specs=placed,
        out_specs=(
            P("expert", "mp"),
            P("expert", None, "mp"),
            P("expert", None, "mp"),
            P("expert", "mp", None),
            P("expert", None),
        ),
        check_vma=False,
    )
```

```python
import functools

import jax
import jax.numpy as jnp
from jax import lax
from jax.experimental import pallas as pl
from jax.experimental.pallas import tpu as pltpu
from jax.sharding import PartitionSpec as P

MESH = pl.DeviceIdType.MESH
F32 = jnp.float32
BF16 = jnp.bfloat16


def nn(a, b):
    return jnp.dot(a, b, preferred_element_type=F32)


def nt(a, b):
    return lax.dot_general(a, b, (((1,), (1,)), ((), ())), preferred_element_type=F32)


def tn(a, b):
    return lax.dot_general(a, b, (((0,), (0,)), ((), ())), preferred_element_type=F32)


def layer_kernel(
    dims,
    x_hbm, cot_hbm, wg_hbm, wu_hbm, wd_hbm, combine_hbm, idx_hbm,
    tokens_ref, terms_ref, grad_gate, grad_up, grad_down,
    rows_in_ref, scaled_ref, act_ref, dgate_ref, dup_ref,
    x_ref, combine_ref, idx_ref, wg, wu, wd, tok, gathered, rx, rows_out, mine, ex_send, ex_recv,
    term_buf, red_send, red_recv, xs_send, xs_recv, bk_send, bk_recv, place,
    w_sem, z_send, z_recv, m_send, m_recv, f_send, x_send, x_recv,
    c_send, c_recv, r_send, r_recv, s_send, s_recv, sf_send, k_send, k_recv,
):
    (groups, lanes, exp_dev, blocks, half_lanes, tok_dev, width, capacity, hidden, chunk, peer) = dims
    half_width = half_lanes * width
    experts = groups * exp_dev
    chunks = hidden // chunk
    z = lax.axis_index("expert")
    lane = lax.axis_index("mp")
    own_b = lax.rem(lane, blocks)
    own_h = lax.rem(lax.div(lane, blocks), 2)
    own_e = lax.div(lane, 2 * blocks)
    feat_half = lax.div(lane, half_lanes)
    feat_pos = lax.rem(lane, half_lanes)

    def lane_of(e, h, b):
        return (e * 2 + h) * blocks + b

    def remote(src, dst, ssem, rsem, to_z, to_lane):
        return pltpu.make_async_remote_copy(
            src_ref=src, dst_ref=dst, send_sem=ssem, recv_sem=rsem,
            device_id=(to_z, to_lane), device_id_type=MESH,
        )

    def arrived(ref, ssem, rsem):
        remote(ref, ref, ssem, rsem, z, lane).wait_recv()

    loads = [
        pltpu.make_async_copy(src, dst, w_sem.at[i])
        for i, (src, dst) in enumerate((
            (idx_hbm, idx_ref), (x_hbm, x_ref), (combine_hbm, combine_ref), (cot_hbm, tok.at[z]),
            (wg_hbm.at[0], wg), (wu_hbm.at[0], wu), (wd_hbm.at[0], wd),
        ))
    ]
    for load in loads:
        load.start()

    barrier = pltpu.get_barrier_semaphore()
    for d in range(1, groups):
        pl.semaphore_signal(barrier, inc=1, device_id=(lax.rem(z + d, groups), lane), device_id_type=MESH)
        for e in range(exp_dev):
            for other in (lane_of(e, feat_half, own_b), own_h * half_lanes + e * blocks + own_b):
                pl.semaphore_signal(barrier, inc=1, device_id=(lax.rem(z + d, groups), other), device_id_type=MESH)
    for d in range(1, lanes):
        pl.semaphore_signal(barrier, inc=1, device_id=(z, lax.rem(lane + d, lanes)), device_id_type=MESH)
    def iota(shape, axis):
        return lax.broadcasted_iota(jnp.int32, shape, axis)

    def before(row, g):
        return jnp.sum(jnp.where((row >= 0) & (row < g * tok_dev), 1.0, 0.0), axis=1, keepdims=True)

    def ones_where(condition):
        return jnp.where(condition, 1.0, 0.0).astype(BF16)

    def token_slot(row):
        return ones_where(iota((tok_dev, capacity), 0) + z * tok_dev == row)

    def row_slot(row, g):
        ahead = iota((peer, capacity), 1) - iota((peer, capacity), 0)
        return ones_where(ahead.astype(F32) == before(row, g))

    loads[0].wait()
    loads[1].wait()
    for d in range(groups):
        g = lax.rem(z + d, groups)
        for e in range(exp_dev):
            row = idx_ref[pl.ds(g * exp_dev + e, 1), :]
            pick = nt(row_slot(row, z), token_slot(row)).astype(BF16)
            xs_send[d, e] = nn(pick, x_ref[...]).astype(BF16)

    pl.semaphore_wait(barrier, lanes - 1 + (groups - 1) * (1 + 2 * exp_dev))

    sends = []

    def send_rows(d, e):
        return remote(xs_send.at[d, e], xs_recv.at[feat_pos, z], s_send.at[d, e], s_recv.at[feat_pos, z],
                      lax.rem(z + d, groups), lane_of(e, feat_half, own_b))

    for d in range(1, groups):
        for e in range(exp_dev):
            copy = send_rows(d, e)
            copy.start()
            sends.append(copy)
    for e in range(exp_dev):
        target = lane_of(e, feat_half, own_b)

        @pl.when(target == lane)
        def _():
            xs_recv[feat_pos, z] = xs_send[0, e]

        @pl.when(target != lane)
        def _():
            send_rows(0, e).start()

    eye = iota((capacity, capacity), 0) == iota((capacity, capacity), 1)

    def column(row):
        return jnp.sum(jnp.where(eye, jnp.broadcast_to(row, (capacity, capacity)), 0.0), axis=1, keepdims=True)

    idx_rows = [idx_ref[pl.ds(z * exp_dev + e, 1), :] for e in range(exp_dev)]
    idx_cols = [column(row.astype(F32)).astype(jnp.int32) for row in idx_rows]
    loads[2].wait()
    weight = column(combine_ref[pl.ds(own_e, 1), :])
    own_row = idx_ref[pl.ds(z * exp_dev + own_e, 1), :]

    def slot_map(axis):
        shape = (capacity, groups * peer) if axis else (groups * peer, capacity)
        spot, slot = iota(shape, axis), iota(shape, 1 - axis)
        total = jnp.zeros(shape, F32)
        for g in range(groups):
            hit = (slot - spot + g * peer).astype(F32) == before(own_row, g)
            total += jnp.where(hit & (spot >= g * peer) & (spot < (g + 1) * peer), 1.0, 0.0)
        return total.astype(BF16)

    to_slots = slot_map(1)
    for d in range(groups):
        zs = lax.rem(z + d, groups)
        for j in range(exp_dev):
            p = j * blocks + own_b
            source = own_h * half_lanes + p

            @pl.when((source != lane) | (d > 0))
            def _():
                arrived(xs_recv.at[p, zs], s_send.at[0, 0], s_recv.at[p, zs])

            for n in range(1, blocks):
                copy = remote(xs_recv.at[p, zs], xs_recv.at[p, zs], sf_send.at[j, zs, n], s_recv.at[p, zs],
                              z, lane_of(own_e, own_h, lax.rem(own_b + n, blocks)))
                copy.start()
                sends.append(copy)

    loads[3].wait()
    for d in range(1, groups):
        copy = remote(tok.at[z], tok.at[z], z_send.at[d], z_recv.at[z], lax.rem(z + d, groups), lane)
        copy.start()
        sends.append(copy)

    for d in range(groups):
        zs = lax.rem(z + d, groups)
        for n in range(1, blocks):
            for j in range(exp_dev):
                p = j * blocks + lax.rem(own_b + n, blocks)
                arrived(xs_recv.at[p, zs], s_send.at[0, 0], s_recv.at[p, zs])
    for p in range(half_lanes):
        packed = xs_recv[p].reshape(groups * peer, width)
        rows_in_ref[:, p * width:(p + 1) * width] = nn(to_slots, packed).astype(BF16)

    def exchange_rows():
        for d in range(1, groups):
            s = lax.rem(z + d, groups)
            arrived(tok.at[s], z_send.at[d], z_recv.at[s])
        for e in range(exp_dev):
            total = jnp.zeros((capacity, width), F32)
            for g in range(groups):
                ids = iota((capacity, tok_dev), 1) + g * tok_dev
                pick = ones_where(ids == idx_cols[e])
                total += nn(pick, tok[g])
            gathered[e] = total.astype(BF16)
            target = lane_of(e, feat_half, own_b)

            @pl.when(target == lane)
            def _():
                rx[feat_pos] = gathered[e]

            @pl.when(target != lane)
            def _():
                remote(gathered.at[e], rx.at[feat_pos], m_send.at[e],
                       m_recv.at[feat_pos], z, target).start()

        for j in range(exp_dev):
            p = j * blocks + own_b
            source = own_h * half_lanes + p

            @pl.when(source != lane)
            def _():
                arrived(rx.at[p], m_send.at[0], m_recv.at[p])

            for d in range(1, blocks):
                copy = remote(rx.at[p], rx.at[p], f_send.at[j, d], m_recv.at[p],
                              z, lane_of(own_e, own_h, lax.rem(own_b + d, blocks)))
                copy.start()
                sends.append(copy)
        for d in range(1, blocks):
            for j in range(exp_dev):
                p = j * blocks + lax.rem(own_b + d, blocks)
                arrived(rx.at[p], m_send.at[0], m_recv.at[p])

    partner = lane_of(own_e, 1 - own_h, own_b)

    def exchange_sum(which, c, value):
        cols = slice(c * chunk, (c + 1) * chunk)
        mine[which, :, cols] = value
        ex_send[which, c] = value.astype(BF16)
        copy = remote(ex_send.at[which, c], ex_recv.at[which, c], x_send.at[which, c],
                      x_recv.at[which, c], z, partner)
        copy.start()
        sends.append(copy)

    loads[4].wait()
    loads[5].wait()
    for c in range(chunks):
        cols = slice(c * chunk, (c + 1) * chunk)
        exchange_sum(0, c, nn(rows_in_ref[...], wg[:, cols]))
        exchange_sum(1, c, nn(rows_in_ref[...], wu[:, cols]))

    exchange_rows()
    for p in range(half_lanes):
        part = rx[p]
        rows_out[:, p * width:(p + 1) * width] = part
        scaled_ref[:, p * width:(p + 1) * width] = (weight * part.astype(F32)).astype(BF16)
    loads[6].wait()
    for c in range(chunks):
        cols = slice(c * chunk, (c + 1) * chunk)
        exchange_sum(2, c, nt(rows_out[...], wd[cols, :]))

    slot_term = jnp.zeros((capacity, 1), F32)
    for c in range(chunks):
        cols = slice(c * chunk, (c + 1) * chunk)
        for which in range(3):
            arrived(ex_recv.at[which, c], x_send.at[which, c], x_recv.at[which, c])
        gate = mine[0, :, cols] + ex_recv[0, c].astype(F32)
        up = mine[1, :, cols] + ex_recv[1, c].astype(F32)
        back = mine[2, :, cols] + ex_recv[2, c].astype(F32)
        s = jax.nn.sigmoid(gate)
        act = (gate * s * up).astype(BF16)
        act_ref[:, cols] = act
        slot_term += jnp.sum(act.astype(F32) * back, axis=1, keepdims=True)
        a = weight * back
        dgate_ref[:, cols] = (a * up * s * (1.0 + gate * (1.0 - s))).astype(BF16)
        dup_ref[:, cols] = (a * gate * s).astype(BF16)

    def block_part(p):
        rows = pl.ds(pl.multiple_of(p * width, width), width)
        return nt(dgate_ref[...], wg[rows, :]) + nt(dup_ref[...], wu[rows, :])

    for d in range(1, blocks):
        to_b = lax.rem(own_b + d, blocks)
        for j in range(exp_dev):
            red_send[d, j] = block_part(j * blocks + to_b).astype(BF16)
            copy = remote(red_send.at[d, j], red_recv.at[own_b, j], r_send.at[d, j], r_recv.at[own_b, j],
                          z, lane_of(own_e, own_h, to_b))
            copy.start()
            sends.append(copy)
    from_slots = slot_map(0)

    def send_back(j, d):
        g = lax.rem(z + d, groups)
        slot = z * exp_dev + own_e
        return remote(bk_send.at[j, g], bk_recv.at[slot], k_send.at[j, d], k_recv.at[slot],
                      g, own_h * half_lanes + j * blocks + own_b)

    for j in range(exp_dev):
        total = block_part(j * blocks + own_b).astype(BF16).astype(F32)
        for d in range(1, blocks):
            from_b = lax.rem(own_b + d, blocks)
            arrived(red_recv.at[from_b, j], r_send.at[d, j], r_recv.at[from_b, j])
            total += red_recv[from_b, j].astype(F32)
        bk_send[j] = nn(from_slots, total.astype(BF16)).astype(BF16).reshape(groups, peer, width)
        for d in range(1, groups):
            copy = send_back(j, d)
            copy.start()
            sends.append(copy)
        target = own_h * half_lanes + j * blocks + own_b

        @pl.when(target == lane)
        def _():
            bk_recv[z * exp_dev + own_e] = bk_send[j, z]

        @pl.when(target != lane)
        def _():
            send_back(j, 0).start()

    term_row = jnp.sum(jnp.where(eye, jnp.broadcast_to(slot_term, (capacity, capacity)), 0.0), axis=0, keepdims=True)

    @pl.when(own_h == 0)
    def _():
        term_buf[own_e, own_b] = jnp.broadcast_to(term_row, (8, capacity))
        for d in range(1, lanes):
            remote(term_buf.at[own_e, own_b], term_buf.at[own_e, own_b], c_send.at[d],
                   c_recv.at[own_e, own_b], z, lax.rem(lane + d, lanes)).start()

    step = min(half_width, 256)
    for i in range(half_width // step):
        cols = slice(i * step, (i + 1) * step)
        grad_gate[0, cols, :] = tn(rows_in_ref[:, cols], dgate_ref[...]).astype(BF16)
        grad_up[0, cols, :] = tn(rows_in_ref[:, cols], dup_ref[...]).astype(BF16)
    for c in range(chunks):
        cols = slice(c * chunk, (c + 1) * chunk)
        grad_down[0, cols, :] = tn(act_ref[:, cols], scaled_ref[...]).astype(BF16)
    for e in range(experts):
        row = idx_ref[e:e + 1, :]
        place[e] = nt(token_slot(row), row_slot(row, z)).astype(BF16)

    for e in range(exp_dev):
        for b in range(blocks):
            @pl.when(lane_of(e, 0, b) != lane)
            def _():
                arrived(term_buf.at[e, b], c_send.at[1], c_recv.at[e, b])
        row = term_buf[e, 0, 0:1, :]
        for b in range(1, blocks):
            row += term_buf[e, b, 0:1, :]
        terms_ref[e:e + 1, :] = row

    total = jnp.zeros((tok_dev, width), F32)
    for d in range(groups):
        zs = lax.rem(z + d, groups)
        for e in range(exp_dev):
            slot = zs * exp_dev + e

            @pl.when((lane_of(e, feat_half, own_b) != lane) | (d > 0))
            def _():
                arrived(bk_recv.at[slot], k_send.at[0, 0], k_recv.at[slot])

            total += nn(place[slot], bk_recv[slot])
    tokens_ref[...] = total.astype(BF16)

    for copy in sends:
        copy.wait_send()
    for e in range(exp_dev):
        target = lane_of(e, feat_half, own_b)

        @pl.when(target != lane)
        def _():
            send_rows(0, e).wait_send()
            remote(gathered.at[e], rx.at[feat_pos], m_send.at[e], m_recv.at[feat_pos], z, target).wait_send()

    for j in range(exp_dev):
        @pl.when(own_h * half_lanes + j * blocks + own_b != lane)
        def _():
            send_back(j, 0).wait_send()

    @pl.when(own_h == 0)
    def _():
        for d in range(1, lanes):
            remote(term_buf.at[own_e, own_b], term_buf.at[own_e, own_b], c_send.at[d],
                   c_recv.at[own_e, own_b], z, lax.rem(lane + d, lanes)).wait_send()


def write_kernel(*refs):
    count = len(refs) // 2
    copies = [
        pltpu.make_async_copy(src, dst, refs[-1].at[i])
        for i, (src, dst) in enumerate(zip(refs[:count], refs[count:2 * count]))
    ]
    for copy in copies:
        copy.start()
    for copy in copies:
        copy.wait()


def local(x_tokens, cotangent, w_gate, w_up, w_down, combine, indices):
    groups = lax.axis_size("expert")
    lanes = lax.axis_size("mp")
    tok_dev, width = x_tokens.shape
    experts, capacity = indices.shape
    exp_dev = experts // groups
    blocks = lanes // (2 * exp_dev)
    half_lanes = lanes // 2
    half_width, hidden = w_gate.shape[1:]
    chunk = min(hidden, 256)
    chunks = hidden // chunk
    peer = max(2 * capacity // groups, 16)
    dims = (groups, lanes, exp_dev, blocks, half_lanes, tok_dev, width, capacity, hidden, chunk, peer)
    vmem = pl.BlockSpec(memory_space=pltpu.VMEM)
    anywhere = pl.BlockSpec(memory_space=pl.ANY)
    dma = pltpu.SemaphoreType.DMA
    slot_half = jax.ShapeDtypeStruct((capacity, half_width), BF16)
    slot_hidden = jax.ShapeDtypeStruct((capacity, hidden), BF16)
    results = [
        jax.ShapeDtypeStruct((tok_dev, width), BF16),
        jax.ShapeDtypeStruct((exp_dev, capacity), F32),
        jax.ShapeDtypeStruct(w_gate.shape, BF16),
        jax.ShapeDtypeStruct(w_up.shape, BF16),
        jax.ShapeDtypeStruct(w_down.shape, BF16),
    ]
    operands = [
        pltpu.with_memory_space_constraint(a, pltpu.HBM)
        for a in (x_tokens, cotangent, w_gate, w_up, w_down, combine, indices)
    ]
    held = pl.pallas_call(
        functools.partial(layer_kernel, dims),
        out_shape=results,
        in_specs=[pl.BlockSpec(memory_space=pltpu.HBM)] * 7,
        out_specs=[vmem] * 5,
        scratch_shapes=[
            pltpu.VMEM((capacity, half_width), BF16),
            pltpu.VMEM((capacity, half_width), BF16),
            pltpu.VMEM((capacity, hidden), BF16),
            pltpu.VMEM((capacity, hidden), BF16),
            pltpu.VMEM((capacity, hidden), BF16),
            pltpu.VMEM((tok_dev, width), BF16),
            pltpu.VMEM((exp_dev, capacity), F32),
            pltpu.VMEM((experts, capacity), jnp.int32),
            pltpu.VMEM((half_width, hidden), BF16),
            pltpu.VMEM((half_width, hidden), BF16),
            pltpu.VMEM((hidden, half_width), BF16),
            pltpu.VMEM((groups, tok_dev, width), BF16),
            pltpu.VMEM((exp_dev, capacity, width), BF16),
            pltpu.VMEM((half_lanes, capacity, width), BF16),
            pltpu.VMEM((capacity, half_width), BF16),
            pltpu.VMEM((3, capacity, hidden), F32),
            pltpu.VMEM((3, chunks, capacity, chunk), BF16),
            pltpu.VMEM((3, chunks, capacity, chunk), BF16),
            pltpu.VMEM((exp_dev, blocks, 8, capacity), F32),
            pltpu.VMEM((blocks, exp_dev, capacity, width), BF16),
            pltpu.VMEM((blocks, exp_dev, capacity, width), BF16),
            pltpu.VMEM((groups, exp_dev, peer, width), BF16),
            pltpu.VMEM((half_lanes, groups, peer, width), BF16),
            pltpu.VMEM((exp_dev, groups, peer, width), BF16),
            pltpu.VMEM((experts, peer, width), BF16),
            pltpu.VMEM((experts, tok_dev, peer), BF16),
            dma((7,)), dma((groups,)), dma((groups,)),
            dma((exp_dev,)), dma((half_lanes,)), dma((exp_dev, blocks)),
            dma((3, chunks)), dma((3, chunks)),
            dma((lanes,)), dma((exp_dev, blocks)),
            dma((blocks, exp_dev)), dma((blocks, exp_dev)),
            dma((groups, exp_dev)), dma((half_lanes, groups)), dma((exp_dev, groups, blocks)),
            dma((exp_dev, groups)), dma((experts,)),
        ],
        compiler_params=pltpu.CompilerParams(
            collective_id=0, has_side_effects=True, vmem_limit_bytes=40 * 1024 * 1024
        ),
        name="layer",
    )(*operands)
    grad_tokens, grad_combine, grad_gate, grad_up, grad_down = pl.pallas_call(
        write_kernel,
        out_shape=results,
        in_specs=[anywhere] * 5,
        out_specs=[anywhere] * 5,
        scratch_shapes=[dma((5,))],
        name="write_out",
    )(*held)
    return grad_tokens, grad_gate, grad_up, grad_down, grad_combine


def solution(mesh):
    placed = (
        P("expert", "mp"),
        P("expert", "mp"),
        P("expert", None, "mp"),
        P("expert", None, "mp"),
        P("expert", "mp", None),
        P("expert", None),
        P(),
    )
    return jax.shard_map(
        local,
        mesh=mesh,
        in_specs=placed,
        out_specs=(
            P("expert", "mp"),
            P("expert", None, "mp"),
            P("expert", None, "mp"),
            P("expert", "mp", None),
            P("expert", None),
        ),
        check_vma=False,
    )
```

```python
import functools

import jax
import jax.numpy as jnp
from jax import lax
from jax.experimental import pallas as pl
from jax.experimental.pallas import tpu as pltpu
from jax.sharding import PartitionSpec as P

MESH = pl.DeviceIdType.MESH
F32 = jnp.float32
BF16 = jnp.bfloat16


def nn(a, b):
    return jnp.dot(a, b, preferred_element_type=F32)


def nt(a, b):
    return lax.dot_general(a, b, (((1,), (1,)), ((), ())), preferred_element_type=F32)


def tn(a, b):
    return lax.dot_general(a, b, (((0,), (0,)), ((), ())), preferred_element_type=F32)


def layer_kernel(
    dims,
    x_hbm, cot_hbm, wg_hbm, wu_hbm, wd_hbm, combine_hbm, idx_hbm,
    tokens_ref, terms_ref, grad_gate, grad_up, grad_down,
    rows_in_ref, scaled_ref, act_ref, dgate_ref, dup_ref,
    x_ref, combine_ref, idx_ref, wg, wu, wd, tok, gathered, rx, rows_out, mine, ex_send, ex_recv,
    term_buf, red_send, red_recv, xs_send, xs_recv, bk_send, bk_recv, place,
    w_sem, z_send, z_recv, m_send, m_recv, f_send, x_send, x_recv,
    c_send, c_recv, r_send, r_recv, s_send, s_recv, sf_send, k_send, k_recv,
):
    (groups, lanes, exp_dev, blocks, half_lanes, tok_dev, width, capacity, hidden, chunk, peer) = dims
    half_width = half_lanes * width
    experts = groups * exp_dev
    chunks = hidden // chunk
    z = lax.axis_index("expert")
    lane = lax.axis_index("mp")
    own_b = lax.rem(lane, blocks)
    own_h = lax.rem(lax.div(lane, blocks), 2)
    own_e = lax.div(lane, 2 * blocks)
    feat_half = lax.div(lane, half_lanes)
    feat_pos = lax.rem(lane, half_lanes)

    def lane_of(e, h, b):
        return (e * 2 + h) * blocks + b

    def remote(src, dst, ssem, rsem, to_z, to_lane):
        return pltpu.make_async_remote_copy(
            src_ref=src, dst_ref=dst, send_sem=ssem, recv_sem=rsem,
            device_id=(to_z, to_lane), device_id_type=MESH,
        )

    def arrived(ref, ssem, rsem):
        remote(ref, ref, ssem, rsem, z, lane).wait_recv()

    loads = [
        pltpu.make_async_copy(src, dst, w_sem.at[i])
        for i, (src, dst) in enumerate((
            (idx_hbm, idx_ref), (x_hbm, x_ref), (combine_hbm, combine_ref), (cot_hbm, tok.at[z]),
            (wg_hbm.at[0], wg), (wu_hbm.at[0], wu), (wd_hbm.at[0], wd),
        ))
    ]
    for load in loads:
        load.start()

    barrier = pltpu.get_barrier_semaphore()
    for d in range(1, groups):
        pl.semaphore_signal(barrier, inc=1, device_id=(lax.rem(z + d, groups), lane), device_id_type=MESH)
        for e in range(exp_dev):
            for other in (lane_of(e, feat_half, own_b), own_h * half_lanes + e * blocks + own_b):
                pl.semaphore_signal(barrier, inc=1, device_id=(lax.rem(z + d, groups), other), device_id_type=MESH)
    for d in range(1, lanes):
        pl.semaphore_signal(barrier, inc=1, device_id=(z, lax.rem(lane + d, lanes)), device_id_type=MESH)
    def iota(shape, axis):
        return lax.broadcasted_iota(jnp.int32, shape, axis)

    def before(row, g):
        return jnp.sum(jnp.where((row >= 0) & (row < g * tok_dev), 1.0, 0.0), axis=1, keepdims=True)

    def ones_where(condition):
        return jnp.where(condition, 1.0, 0.0).astype(BF16)

    def token_slot(row):
        return ones_where(iota((tok_dev, capacity), 0) + z * tok_dev == row)

    def row_slot(row, g):
        ahead = iota((peer, capacity), 1) - iota((peer, capacity), 0)
        return ones_where(ahead.astype(F32) == before(row, g))

    loads[0].wait()
    loads[1].wait()
    for d in range(groups):
        g = lax.rem(z + d, groups)
        for e in range(exp_dev):
            row = idx_ref[pl.ds(g * exp_dev + e, 1), :]
            pick = nt(row_slot(row, z), token_slot(row)).astype(BF16)
            xs_send[d, e] = nn(pick, x_ref[...]).astype(BF16)

    pl.semaphore_wait(barrier, lanes - 1 + (groups - 1) * (1 + 2 * exp_dev))

    sends = []

    def send_rows(d, e):
        return remote(xs_send.at[d, e], xs_recv.at[feat_pos, z], s_send.at[d, e], s_recv.at[feat_pos, z],
                      lax.rem(z + d, groups), lane_of(e, feat_half, own_b))

    for d in range(1, groups):
        for e in range(exp_dev):
            copy = send_rows(d, e)
            copy.start()
            sends.append(copy)
    for e in range(exp_dev):
        target = lane_of(e, feat_half, own_b)

        @pl.when(target == lane)
        def _():
            xs_recv[feat_pos, z] = xs_send[0, e]

        @pl.when(target != lane)
        def _():
            send_rows(0, e).start()

    eye = iota((capacity, capacity), 0) == iota((capacity, capacity), 1)

    def column(row):
        return jnp.sum(jnp.where(eye, jnp.broadcast_to(row, (capacity, capacity)), 0.0), axis=1, keepdims=True)

    idx_rows = [idx_ref[pl.ds(z * exp_dev + e, 1), :] for e in range(exp_dev)]
    idx_cols = [column(row.astype(F32)).astype(jnp.int32) for row in idx_rows]
    loads[2].wait()
    weight = column(combine_ref[pl.ds(own_e, 1), :])
    own_row = idx_ref[pl.ds(z * exp_dev + own_e, 1), :]

    def slot_map(axis):
        shape = (capacity, groups * peer) if axis else (groups * peer, capacity)
        spot, slot = iota(shape, axis), iota(shape, 1 - axis)
        total = jnp.zeros(shape, F32)
        for g in range(groups):
            hit = (slot - spot + g * peer).astype(F32) == before(own_row, g)
            total += jnp.where(hit & (spot >= g * peer) & (spot < (g + 1) * peer), 1.0, 0.0)
        return total.astype(BF16)

    to_slots = slot_map(1)
    for d in range(groups):
        zs = lax.rem(z + d, groups)
        for j in range(exp_dev):
            p = j * blocks + own_b
            source = own_h * half_lanes + p

            @pl.when((source != lane) | (d > 0))
            def _():
                arrived(xs_recv.at[p, zs], s_send.at[0, 0], s_recv.at[p, zs])

            for n in range(1, blocks):
                copy = remote(xs_recv.at[p, zs], xs_recv.at[p, zs], sf_send.at[j, zs, n], s_recv.at[p, zs],
                              z, lane_of(own_e, own_h, lax.rem(own_b + n, blocks)))
                copy.start()
                sends.append(copy)

    loads[3].wait()
    for d in range(1, groups):
        copy = remote(tok.at[z], tok.at[z], z_send.at[d], z_recv.at[z], lax.rem(z + d, groups), lane)
        copy.start()
        sends.append(copy)

    for d in range(groups):
        zs = lax.rem(z + d, groups)
        for n in range(1, blocks):
            for j in range(exp_dev):
                p = j * blocks + lax.rem(own_b + n, blocks)
                arrived(xs_recv.at[p, zs], s_send.at[0, 0], s_recv.at[p, zs])
    for p in range(half_lanes):
        packed = xs_recv[p].reshape(groups * peer, width)
        rows_in_ref[:, p * width:(p + 1) * width] = nn(to_slots, packed).astype(BF16)

    def exchange_rows():
        for d in range(1, groups):
            s = lax.rem(z + d, groups)
            arrived(tok.at[s], z_send.at[d], z_recv.at[s])
        for e in range(exp_dev):
            total = jnp.zeros((capacity, width), F32)
            for g in range(groups):
                ids = iota((capacity, tok_dev), 1) + g * tok_dev
                pick = ones_where(ids == idx_cols[e])
                total += nn(pick, tok[g])
            gathered[e] = total.astype(BF16)
            target = lane_of(e, feat_half, own_b)

            @pl.when(target == lane)
            def _():
                rx[feat_pos] = gathered[e]

            @pl.when(target != lane)
            def _():
                remote(gathered.at[e], rx.at[feat_pos], m_send.at[e],
                       m_recv.at[feat_pos], z, target).start()

        for j in range(exp_dev):
            p = j * blocks + own_b
            source = own_h * half_lanes + p

            @pl.when(source != lane)
            def _():
                arrived(rx.at[p], m_send.at[0], m_recv.at[p])

            for d in range(1, blocks):
                copy = remote(rx.at[p], rx.at[p], f_send.at[j, d], m_recv.at[p],
                              z, lane_of(own_e, own_h, lax.rem(own_b + d, blocks)))
                copy.start()
                sends.append(copy)
        for d in range(1, blocks):
            for j in range(exp_dev):
                p = j * blocks + lax.rem(own_b + d, blocks)
                arrived(rx.at[p], m_send.at[0], m_recv.at[p])

    partner = lane_of(own_e, 1 - own_h, own_b)

    def exchange_sum(which, c, value):
        cols = slice(c * chunk, (c + 1) * chunk)
        mine[which, :, cols] = value
        ex_send[which, c] = value.astype(BF16)
        copy = remote(ex_send.at[which, c], ex_recv.at[which, c], x_send.at[which, c],
                      x_recv.at[which, c], z, partner)
        copy.start()
        sends.append(copy)

    loads[4].wait()
    loads[5].wait()
    for c in range(chunks):
        cols = slice(c * chunk, (c + 1) * chunk)
        exchange_sum(0, c, nn(rows_in_ref[...], wg[:, cols]))
        exchange_sum(1, c, nn(rows_in_ref[...], wu[:, cols]))

    exchange_rows()
    for p in range(half_lanes):
        part = rx[p]
        rows_out[:, p * width:(p + 1) * width] = part
        scaled_ref[:, p * width:(p + 1) * width] = (weight * part.astype(F32)).astype(BF16)
    loads[6].wait()
    for c in range(chunks):
        cols = slice(c * chunk, (c + 1) * chunk)
        exchange_sum(2, c, nt(rows_out[...], wd[cols, :]))

    slot_term = jnp.zeros((capacity, 1), F32)
    for c in range(chunks):
        cols = slice(c * chunk, (c + 1) * chunk)
        for which in range(3):
            arrived(ex_recv.at[which, c], x_send.at[which, c], x_recv.at[which, c])
        gate = mine[0, :, cols] + ex_recv[0, c].astype(F32)
        up = mine[1, :, cols] + ex_recv[1, c].astype(F32)
        back = mine[2, :, cols] + ex_recv[2, c].astype(F32)
        s = jax.nn.sigmoid(gate)
        act = (gate * s * up).astype(BF16)
        act_ref[:, cols] = act
        slot_term += jnp.sum(act.astype(F32) * back, axis=1, keepdims=True)
        a = weight * back
        dgate_ref[:, cols] = (a * up * s * (1.0 + gate * (1.0 - s))).astype(BF16)
        dup_ref[:, cols] = (a * gate * s).astype(BF16)

    def block_part(p):
        rows = pl.ds(pl.multiple_of(p * width, width), width)
        return nt(dgate_ref[...], wg[rows, :]) + nt(dup_ref[...], wu[rows, :])

    for d in range(1, blocks):
        to_b = lax.rem(own_b + d, blocks)
        for j in range(exp_dev):
            red_send[d, j] = block_part(j * blocks + to_b).astype(BF16)
            copy = remote(red_send.at[d, j], red_recv.at[own_b, j], r_send.at[d, j], r_recv.at[own_b, j],
                          z, lane_of(own_e, own_h, to_b))
            copy.start()
            sends.append(copy)
    from_slots = slot_map(0)

    def send_back(j, d):
        g = lax.rem(z + d, groups)
        slot = z * exp_dev + own_e
        return remote(bk_send.at[j, g], bk_recv.at[slot], k_send.at[j, d], k_recv.at[slot],
                      g, own_h * half_lanes + j * blocks + own_b)

    for j in range(exp_dev):
        total = block_part(j * blocks + own_b).astype(BF16).astype(F32)
        for d in range(1, blocks):
            from_b = lax.rem(own_b + d, blocks)
            arrived(red_recv.at[from_b, j], r_send.at[d, j], r_recv.at[from_b, j])
            total += red_recv[from_b, j].astype(F32)
        bk_send[j] = nn(from_slots, total.astype(BF16)).astype(BF16).reshape(groups, peer, width)
        for d in range(1, groups):
            copy = send_back(j, d)
            copy.start()
            sends.append(copy)
        target = own_h * half_lanes + j * blocks + own_b

        @pl.when(target == lane)
        def _():
            bk_recv[z * exp_dev + own_e] = bk_send[j, z]

        @pl.when(target != lane)
        def _():
            send_back(j, 0).start()

    term_row = jnp.sum(jnp.where(eye, jnp.broadcast_to(slot_term, (capacity, capacity)), 0.0), axis=0, keepdims=True)

    @pl.when(own_h == 0)
    def _():
        term_buf[own_e, own_b] = jnp.broadcast_to(term_row, (8, capacity))
        for d in range(1, lanes):
            remote(term_buf.at[own_e, own_b], term_buf.at[own_e, own_b], c_send.at[d],
                   c_recv.at[own_e, own_b], z, lax.rem(lane + d, lanes)).start()

    step = min(half_width, 256)
    for i in range(half_width // step):
        cols = slice(i * step, (i + 1) * step)
        grad_gate[0, cols, :] = tn(rows_in_ref[:, cols], dgate_ref[...]).astype(BF16)
        grad_up[0, cols, :] = tn(rows_in_ref[:, cols], dup_ref[...]).astype(BF16)
    for c in range(chunks):
        cols = slice(c * chunk, (c + 1) * chunk)
        grad_down[0, cols, :] = tn(act_ref[:, cols], scaled_ref[...]).astype(BF16)
    for e in range(experts):
        row = idx_ref[e:e + 1, :]
        place[e] = nt(token_slot(row), row_slot(row, z)).astype(BF16)

    for e in range(exp_dev):
        for b in range(blocks):
            @pl.when(lane_of(e, 0, b) != lane)
            def _():
                arrived(term_buf.at[e, b], c_send.at[1], c_recv.at[e, b])
        row = term_buf[e, 0, 0:1, :]
        for b in range(1, blocks):
            row += term_buf[e, b, 0:1, :]
        terms_ref[e:e + 1, :] = row

    total = jnp.zeros((tok_dev, width), F32)
    for d in range(groups):
        zs = lax.rem(z + d, groups)
        for e in range(exp_dev):
            slot = zs * exp_dev + e

            @pl.when((lane_of(e, feat_half, own_b) != lane) | (d > 0))
            def _():
                arrived(bk_recv.at[slot], k_send.at[0, 0], k_recv.at[slot])

            total += nn(place[slot], bk_recv[slot])
    tokens_ref[...] = total.astype(BF16)

    for copy in sends:
        copy.wait_send()
    for e in range(exp_dev):
        target = lane_of(e, feat_half, own_b)

        @pl.when(target != lane)
        def _():
            send_rows(0, e).wait_send()
            remote(gathered.at[e], rx.at[feat_pos], m_send.at[e], m_recv.at[feat_pos], z, target).wait_send()

    for j in range(exp_dev):
        @pl.when(own_h * half_lanes + j * blocks + own_b != lane)
        def _():
            send_back(j, 0).wait_send()

    @pl.when(own_h == 0)
    def _():
        for d in range(1, lanes):
            remote(term_buf.at[own_e, own_b], term_buf.at[own_e, own_b], c_send.at[d],
                   c_recv.at[own_e, own_b], z, lax.rem(lane + d, lanes)).wait_send()


def write_kernel(*refs):
    count = len(refs) // 2
    copies = [
        pltpu.make_async_copy(src, dst, refs[-1].at[i])
        for i, (src, dst) in enumerate(zip(refs[:count], refs[count:2 * count]))
    ]
    for copy in copies:
        copy.start()
    for copy in copies:
        copy.wait()


def local(x_tokens, cotangent, w_gate, w_up, w_down, combine, indices):
    groups = lax.axis_size("expert")
    lanes = lax.axis_size("mp")
    tok_dev, width = x_tokens.shape
    experts, capacity = indices.shape
    exp_dev = experts // groups
    blocks = lanes // (2 * exp_dev)
    half_lanes = lanes // 2
    half_width, hidden = w_gate.shape[1:]
    chunk = min(hidden, 256)
    chunks = hidden // chunk
    peer = max(2 * capacity // groups, 16)
    dims = (groups, lanes, exp_dev, blocks, half_lanes, tok_dev, width, capacity, hidden, chunk, peer)
    vmem = pl.BlockSpec(memory_space=pltpu.VMEM)
    anywhere = pl.BlockSpec(memory_space=pl.ANY)
    dma = pltpu.SemaphoreType.DMA
    slot_half = jax.ShapeDtypeStruct((capacity, half_width), BF16)
    slot_hidden = jax.ShapeDtypeStruct((capacity, hidden), BF16)
    results = [
        jax.ShapeDtypeStruct((tok_dev, width), BF16),
        jax.ShapeDtypeStruct((exp_dev, capacity), F32),
        jax.ShapeDtypeStruct(w_gate.shape, BF16),
        jax.ShapeDtypeStruct(w_up.shape, BF16),
        jax.ShapeDtypeStruct(w_down.shape, BF16),
    ]
    operands = [
        pltpu.with_memory_space_constraint(a, pltpu.HBM)
        for a in (x_tokens, cotangent, w_gate, w_up, w_down, combine, indices)
    ]
    held = pl.pallas_call(
        functools.partial(layer_kernel, dims),
        out_shape=results,
        in_specs=[pl.BlockSpec(memory_space=pltpu.HBM)] * 7,
        out_specs=[vmem] * 5,
        scratch_shapes=[
            pltpu.VMEM((capacity, half_width), BF16),
            pltpu.VMEM((capacity, half_width), BF16),
            pltpu.VMEM((capacity, hidden), BF16),
            pltpu.VMEM((capacity, hidden), BF16),
            pltpu.VMEM((capacity, hidden), BF16),
            pltpu.VMEM((tok_dev, width), BF16),
            pltpu.VMEM((exp_dev, capacity), F32),
            pltpu.VMEM((experts, capacity), jnp.int32),
            pltpu.VMEM((half_width, hidden), BF16),
            pltpu.VMEM((half_width, hidden), BF16),
            pltpu.VMEM((hidden, half_width), BF16),
            pltpu.VMEM((groups, tok_dev, width), BF16),
            pltpu.VMEM((exp_dev, capacity, width), BF16),
            pltpu.VMEM((half_lanes, capacity, width), BF16),
            pltpu.VMEM((capacity, half_width), BF16),
            pltpu.VMEM((3, capacity, hidden), F32),
            pltpu.VMEM((3, chunks, capacity, chunk), BF16),
            pltpu.VMEM((3, chunks, capacity, chunk), BF16),
            pltpu.VMEM((exp_dev, blocks, 8, capacity), F32),
            pltpu.VMEM((blocks, exp_dev, capacity, width), BF16),
            pltpu.VMEM((blocks, exp_dev, capacity, width), BF16),
            pltpu.VMEM((groups, exp_dev, peer, width), BF16),
            pltpu.VMEM((half_lanes, groups, peer, width), BF16),
            pltpu.VMEM((exp_dev, groups, peer, width), BF16),
            pltpu.VMEM((experts, peer, width), BF16),
            pltpu.VMEM((experts, tok_dev, peer), BF16),
            dma((7,)), dma((groups,)), dma((groups,)),
            dma((exp_dev,)), dma((half_lanes,)), dma((exp_dev, blocks)),
            dma((3, chunks)), dma((3, chunks)),
            dma((lanes,)), dma((exp_dev, blocks)),
            dma((blocks, exp_dev)), dma((blocks, exp_dev)),
            dma((groups, exp_dev)), dma((half_lanes, groups)), dma((exp_dev, groups, blocks)),
            dma((exp_dev, groups)), dma((experts,)),
        ],
        compiler_params=pltpu.CompilerParams(
            collective_id=0, has_side_effects=True, vmem_limit_bytes=40 * 1024 * 1024
        ),
        name="layer",
    )(*operands)
    grad_tokens, grad_combine, grad_gate, grad_up, grad_down = pl.pallas_call(
        write_kernel,
        out_shape=results,
        in_specs=[anywhere] * 5,
        out_specs=[anywhere] * 5,
        scratch_shapes=[dma((5,))],
        compiler_params=pltpu.CompilerParams(vmem_limit_bytes=1024 * 1024),
        name="write_out",
    )(*[pltpu.with_memory_space_constraint(a, pltpu.VMEM) for a in held])
    return grad_tokens, grad_gate, grad_up, grad_down, grad_combine


def solution(mesh):
    placed = (
        P("expert", "mp"),
        P("expert", "mp"),
        P("expert", None, "mp"),
        P("expert", None, "mp"),
        P("expert", "mp", None),
        P("expert", None),
        P(),
    )
    return jax.shard_map(
        local,
        mesh=mesh,
        in_specs=placed,
        out_specs=(
            P("expert", "mp"),
            P("expert", None, "mp"),
            P("expert", None, "mp"),
            P("expert", "mp", None),
            P("expert", None),
        ),
        check_vma=False,
    )
```

```python
import functools

import jax
import jax.numpy as jnp
from jax import lax
from jax.experimental import pallas as pl
from jax.experimental.pallas import tpu as pltpu
from jax.sharding import PartitionSpec as P

MESH = pl.DeviceIdType.MESH
F32 = jnp.float32
BF16 = jnp.bfloat16


def nn(a, b):
    return jnp.dot(a, b, preferred_element_type=F32)


def nt(a, b):
    return lax.dot_general(a, b, (((1,), (1,)), ((), ())), preferred_element_type=F32)


def tn(a, b):
    return lax.dot_general(a, b, (((0,), (0,)), ((), ())), preferred_element_type=F32)


def layer_kernel(
    dims,
    x_hbm, cot_hbm, wg_hbm, wu_hbm, wd_hbm, combine_hbm, idx_hbm,
    tokens_ref, terms_ref, grad_gate, grad_up, grad_down,
    rows_in_ref, scaled_ref, act_ref, dgate_ref, dup_ref,
    x_ref, cot_ref, combine_ref, idx_ref, wg, wu, wd, rows_out, mine, ex_send, ex_recv,
    term_buf, red_send, red_recv, xs_send, xs_recv, bk_send, bk_recv, place, acc,
    w_sem, x_send, x_recv,
    c_send, c_recv, r_send, r_recv, s_send, s_recv, sf_send, k_send, k_recv,
):
    (groups, lanes, exp_dev, blocks, half_lanes, tok_dev, width, capacity, hidden, chunk, peer) = dims
    half_width = half_lanes * width
    experts = groups * exp_dev
    chunks = hidden // chunk
    z = lax.axis_index("expert")
    lane = lax.axis_index("mp")
    own_b = lax.rem(lane, blocks)
    own_h = lax.rem(lax.div(lane, blocks), 2)
    own_e = lax.div(lane, 2 * blocks)
    feat_half = lax.div(lane, half_lanes)
    feat_pos = lax.rem(lane, half_lanes)

    def lane_of(e, h, b):
        return (e * 2 + h) * blocks + b

    def remote(src, dst, ssem, rsem, to_z, to_lane):
        return pltpu.make_async_remote_copy(
            src_ref=src, dst_ref=dst, send_sem=ssem, recv_sem=rsem,
            device_id=(to_z, to_lane), device_id_type=MESH,
        )

    def arrived(ref, ssem, rsem):
        remote(ref, ref, ssem, rsem, z, lane).wait_recv()

    loads = [
        pltpu.make_async_copy(src, dst, w_sem.at[i])
        for i, (src, dst) in enumerate((
            (idx_hbm, idx_ref), (x_hbm, x_ref), (combine_hbm, combine_ref), (cot_hbm, cot_ref),
            (wg_hbm.at[0], wg), (wu_hbm.at[0], wu), (wd_hbm.at[0], wd),
        ))
    ]
    for load in loads:
        load.start()

    barrier = pltpu.get_barrier_semaphore()
    for d in range(1, groups):
        pl.semaphore_signal(barrier, inc=1, device_id=(lax.rem(z + d, groups), lane), device_id_type=MESH)
        for e in range(exp_dev):
            for other in (lane_of(e, feat_half, own_b), own_h * half_lanes + e * blocks + own_b):
                pl.semaphore_signal(barrier, inc=1, device_id=(lax.rem(z + d, groups), other), device_id_type=MESH)
    for d in range(1, lanes):
        pl.semaphore_signal(barrier, inc=1, device_id=(z, lax.rem(lane + d, lanes)), device_id_type=MESH)
    def iota(shape, axis):
        return lax.broadcasted_iota(jnp.int32, shape, axis)

    def before(row, g):
        return jnp.sum(jnp.where((row >= 0) & (row < g * tok_dev), 1.0, 0.0), axis=1, keepdims=True)

    def ones_where(condition):
        return jnp.where(condition, 1.0, 0.0).astype(BF16)

    def token_slot(row):
        return ones_where(iota((tok_dev, capacity), 0) + z * tok_dev == row)

    def row_slot(row, g):
        ahead = iota((peer, capacity), 1) - iota((peer, capacity), 0)
        return ones_where(ahead.astype(F32) == before(row, g))

    loads[0].wait()
    loads[1].wait()
    loads[3].wait()
    for d in range(groups):
        g = lax.rem(z + d, groups)
        for e in range(exp_dev):
            row = idx_ref[pl.ds(g * exp_dev + e, 1), :]
            pick = nt(row_slot(row, z), token_slot(row)).astype(BF16)
            xs_send[0, d, e] = nn(pick, x_ref[...]).astype(BF16)
            xs_send[1, d, e] = nn(pick, cot_ref[...]).astype(BF16)

    pl.semaphore_wait(barrier, lanes - 1 + (groups - 1) * (1 + 2 * exp_dev))

    sends = []

    def send_rows(kind, d, e):
        return remote(xs_send.at[kind, d, e], xs_recv.at[kind, feat_pos, z], s_send.at[kind, d, e],
                      s_recv.at[kind, feat_pos, z], lax.rem(z + d, groups), lane_of(e, feat_half, own_b))

    def start_rows(kind):
        for d in range(1, groups):
            for e in range(exp_dev):
                send_rows(kind, d, e).start()
        for e in range(exp_dev):
            target = lane_of(e, feat_half, own_b)

            @pl.when(target == lane)
            def _():
                xs_recv[kind, feat_pos, z] = xs_send[kind, 0, e]

            @pl.when(target != lane)
            def _():
                send_rows(kind, 0, e).start()

    def finish_rows(kind):
        for d in range(1, groups):
            for e in range(exp_dev):
                send_rows(kind, d, e).wait_send()
        for e in range(exp_dev):
            @pl.when(lane_of(e, feat_half, own_b) != lane)
            def _():
                send_rows(kind, 0, e).wait_send()

    start_rows(0)

    eye = iota((capacity, capacity), 0) == iota((capacity, capacity), 1)

    def column(row):
        return jnp.sum(jnp.where(eye, jnp.broadcast_to(row, (capacity, capacity)), 0.0), axis=1, keepdims=True)

    loads[2].wait()
    weight = column(combine_ref[pl.ds(own_e, 1), :])
    own_row = idx_ref[pl.ds(z * exp_dev + own_e, 1), :]

    def slot_map(axis):
        shape = (capacity, groups * peer) if axis else (groups * peer, capacity)
        spot, slot = iota(shape, axis), iota(shape, 1 - axis)
        total = jnp.zeros(shape, F32)
        for g in range(groups):
            hit = (slot - spot + g * peer).astype(F32) == before(own_row, g)
            total += jnp.where(hit & (spot >= g * peer) & (spot < (g + 1) * peer), 1.0, 0.0)
        return total.astype(BF16)

    to_slots = slot_map(1)

    def arrive_rows(kind, rows_ref):
        for d in range(groups):
            zs = lax.rem(z + d, groups)
            for j in range(exp_dev):
                p = j * blocks + own_b
                source = own_h * half_lanes + p

                @pl.when((source != lane) | (d > 0))
                def _():
                    arrived(xs_recv.at[kind, p, zs], s_send.at[kind, 0, 0], s_recv.at[kind, p, zs])

                for n in range(1, blocks):
                    copy = remote(xs_recv.at[kind, p, zs], xs_recv.at[kind, p, zs], sf_send.at[kind, j, zs, n],
                                  s_recv.at[kind, p, zs], z, lane_of(own_e, own_h, lax.rem(own_b + n, blocks)))
                    copy.start()
                    sends.append(copy)
        for d in range(groups):
            zs = lax.rem(z + d, groups)
            for n in range(1, blocks):
                for j in range(exp_dev):
                    p = j * blocks + lax.rem(own_b + n, blocks)
                    arrived(xs_recv.at[kind, p, zs], s_send.at[kind, 0, 0], s_recv.at[kind, p, zs])
        for p in range(half_lanes):
            packed = xs_recv[kind, p].reshape(groups * peer, width)
            rows_ref[:, p * width:(p + 1) * width] = nn(to_slots, packed).astype(BF16)

    finish_rows(0)
    start_rows(1)
    arrive_rows(0, rows_in_ref)

    partner = lane_of(own_e, 1 - own_h, own_b)

    def exchange_sum(which, c, value):
        cols = slice(c * chunk, (c + 1) * chunk)
        mine[which, :, cols] = value
        ex_send[which, c] = value.astype(BF16)
        copy = remote(ex_send.at[which, c], ex_recv.at[which, c], x_send.at[which, c],
                      x_recv.at[which, c], z, partner)
        copy.start()
        sends.append(copy)

    loads[4].wait()
    loads[5].wait()
    for c in range(chunks):
        cols = slice(c * chunk, (c + 1) * chunk)
        exchange_sum(0, c, nn(rows_in_ref[...], wg[:, cols]))
        exchange_sum(1, c, nn(rows_in_ref[...], wu[:, cols]))

    arrive_rows(1, rows_out)
    scaled_ref[...] = (weight * rows_out[...].astype(F32)).astype(BF16)
    loads[6].wait()
    for c in range(chunks):
        cols = slice(c * chunk, (c + 1) * chunk)
        exchange_sum(2, c, nt(rows_out[...], wd[cols, :]))

    def sum_arrived(which, c):
        arrived(ex_recv.at[which, c], x_send.at[which, c], x_recv.at[which, c])
        return mine[which, :, c * chunk:(c + 1) * chunk] + ex_recv[which, c].astype(F32)

    for c in range(chunks):
        cols = slice(c * chunk, (c + 1) * chunk)
        gate = sum_arrived(0, c)
        up = sum_arrived(1, c)
        s = jax.nn.sigmoid(gate)
        swish = gate * s
        act_ref[:, cols] = (swish * up).astype(BF16)
        mine[0, :, cols] = up * s * (1.0 + gate * (1.0 - s))
        mine[1, :, cols] = swish
        grad_down[0, cols, :] = tn(act_ref[:, cols], scaled_ref[...]).astype(BF16)

    def part_of(p, cols):
        rows = pl.ds(pl.multiple_of(p * width, width), width)
        return nt(dgate_ref[:, cols], wg[rows, cols]) + nt(dup_ref[:, cols], wu[rows, cols])

    slot_term = jnp.zeros((capacity, 1), F32)
    for c in range(chunks):
        cols = slice(c * chunk, (c + 1) * chunk)
        back = sum_arrived(2, c)
        slot_term += jnp.sum(act_ref[:, cols].astype(F32) * back, axis=1, keepdims=True)
        a = weight * back
        dgate_ref[:, cols] = (a * mine[0, :, cols]).astype(BF16)
        dup_ref[:, cols] = (a * mine[1, :, cols]).astype(BF16)
        if c < chunks - 1:
            for p in range(half_lanes):
                if c == 0:
                    acc[p] = part_of(p, cols)
                else:
                    acc[p] += part_of(p, cols)

    def block_part(p):
        last = part_of(p, slice((chunks - 1) * chunk, hidden))
        return acc[p] + last if chunks > 1 else last

    for d in range(1, blocks):
        to_b = lax.rem(own_b + d, blocks)
        for j in range(exp_dev):
            red_send[d, j] = block_part(j * blocks + to_b).astype(BF16)
            copy = remote(red_send.at[d, j], red_recv.at[own_b, j], r_send.at[d, j], r_recv.at[own_b, j],
                          z, lane_of(own_e, own_h, to_b))
            copy.start()
            sends.append(copy)
    from_slots = slot_map(0)

    def send_back(j, d):
        g = lax.rem(z + d, groups)
        slot = z * exp_dev + own_e
        return remote(bk_send.at[j, g], bk_recv.at[slot], k_send.at[j, d], k_recv.at[slot],
                      g, own_h * half_lanes + j * blocks + own_b)

    for j in range(exp_dev):
        total = block_part(j * blocks + own_b).astype(BF16).astype(F32)
        for d in range(1, blocks):
            from_b = lax.rem(own_b + d, blocks)
            arrived(red_recv.at[from_b, j], r_send.at[d, j], r_recv.at[from_b, j])
            total += red_recv[from_b, j].astype(F32)
        bk_send[j] = nn(from_slots, total.astype(BF16)).astype(BF16).reshape(groups, peer, width)
        for d in range(1, groups):
            copy = send_back(j, d)
            copy.start()
            sends.append(copy)
        target = own_h * half_lanes + j * blocks + own_b

        @pl.when(target == lane)
        def _():
            bk_recv[z * exp_dev + own_e] = bk_send[j, z]

        @pl.when(target != lane)
        def _():
            send_back(j, 0).start()

    term_row = jnp.sum(jnp.where(eye, jnp.broadcast_to(slot_term, (capacity, capacity)), 0.0), axis=0, keepdims=True)

    @pl.when(own_h == 0)
    def _():
        term_buf[own_e, own_b] = jnp.broadcast_to(term_row, (8, capacity))
        for d in range(1, lanes):
            remote(term_buf.at[own_e, own_b], term_buf.at[own_e, own_b], c_send.at[d],
                   c_recv.at[own_e, own_b], z, lax.rem(lane + d, lanes)).start()

    step = min(half_width, 256)
    for i in range(half_width // step):
        cols = slice(i * step, (i + 1) * step)
        grad_gate[0, cols, :] = tn(rows_in_ref[:, cols], dgate_ref[...]).astype(BF16)
        grad_up[0, cols, :] = tn(rows_in_ref[:, cols], dup_ref[...]).astype(BF16)
    for e in range(experts):
        row = idx_ref[e:e + 1, :]
        place[e] = nt(token_slot(row), row_slot(row, z)).astype(BF16)

    for e in range(exp_dev):
        for b in range(blocks):
            @pl.when(lane_of(e, 0, b) != lane)
            def _():
                arrived(term_buf.at[e, b], c_send.at[1], c_recv.at[e, b])
        row = term_buf[e, 0, 0:1, :]
        for b in range(1, blocks):
            row += term_buf[e, b, 0:1, :]
        terms_ref[e:e + 1, :] = row

    total = jnp.zeros((tok_dev, width), F32)
    for d in range(groups):
        zs = lax.rem(z + d, groups)
        for e in range(exp_dev):
            slot = zs * exp_dev + e

            @pl.when((lane_of(e, feat_half, own_b) != lane) | (d > 0))
            def _():
                arrived(bk_recv.at[slot], k_send.at[0, 0], k_recv.at[slot])

            total += nn(place[slot], bk_recv[slot])
    tokens_ref[...] = total.astype(BF16)

    for copy in sends:
        copy.wait_send()
    finish_rows(1)
    for j in range(exp_dev):
        @pl.when(own_h * half_lanes + j * blocks + own_b != lane)
        def _():
            send_back(j, 0).wait_send()

    @pl.when(own_h == 0)
    def _():
        for d in range(1, lanes):
            remote(term_buf.at[own_e, own_b], term_buf.at[own_e, own_b], c_send.at[d],
                   c_recv.at[own_e, own_b], z, lax.rem(lane + d, lanes)).wait_send()


def write_kernel(*refs):
    count = len(refs) // 2
    copies = [
        pltpu.make_async_copy(src, dst, refs[-1].at[i])
        for i, (src, dst) in enumerate(zip(refs[:count], refs[count:2 * count]))
    ]
    for copy in copies:
        copy.start()
    for copy in copies:
        copy.wait()


def local(x_tokens, cotangent, w_gate, w_up, w_down, combine, indices):
    groups = lax.axis_size("expert")
    lanes = lax.axis_size("mp")
    tok_dev, width = x_tokens.shape
    experts, capacity = indices.shape
    exp_dev = experts // groups
    blocks = lanes // (2 * exp_dev)
    half_lanes = lanes // 2
    half_width, hidden = w_gate.shape[1:]
    chunk = min(hidden, 256)
    chunks = hidden // chunk
    peer = max(2 * capacity // groups, 16)
    dims = (groups, lanes, exp_dev, blocks, half_lanes, tok_dev, width, capacity, hidden, chunk, peer)
    vmem = pl.BlockSpec(memory_space=pltpu.VMEM)
    anywhere = pl.BlockSpec(memory_space=pl.ANY)
    dma = pltpu.SemaphoreType.DMA
    slot_half = jax.ShapeDtypeStruct((capacity, half_width), BF16)
    slot_hidden = jax.ShapeDtypeStruct((capacity, hidden), BF16)
    results = [
        jax.ShapeDtypeStruct((tok_dev, width), BF16),
        jax.ShapeDtypeStruct((exp_dev, capacity), F32),
        jax.ShapeDtypeStruct(w_gate.shape, BF16),
        jax.ShapeDtypeStruct(w_up.shape, BF16),
        jax.ShapeDtypeStruct(w_down.shape, BF16),
    ]
    operands = [
        pltpu.with_memory_space_constraint(a, pltpu.HBM)
        for a in (x_tokens, cotangent, w_gate, w_up, w_down, combine, indices)
    ]
    held = pl.pallas_call(
        functools.partial(layer_kernel, dims),
        out_shape=results,
        in_specs=[pl.BlockSpec(memory_space=pltpu.HBM)] * 7,
        out_specs=[vmem] * 5,
        scratch_shapes=[
            pltpu.VMEM((capacity, half_width), BF16),
            pltpu.VMEM((capacity, half_width), BF16),
            pltpu.VMEM((capacity, hidden), BF16),
            pltpu.VMEM((capacity, hidden), BF16),
            pltpu.VMEM((capacity, hidden), BF16),
            pltpu.VMEM((tok_dev, width), BF16),
            pltpu.VMEM((tok_dev, width), BF16),
            pltpu.VMEM((exp_dev, capacity), F32),
            pltpu.VMEM((experts, capacity), jnp.int32),
            pltpu.VMEM((half_width, hidden), BF16),
            pltpu.VMEM((half_width, hidden), BF16),
            pltpu.VMEM((hidden, half_width), BF16),
            pltpu.VMEM((capacity, half_width), BF16),
            pltpu.VMEM((3, capacity, hidden), F32),
            pltpu.VMEM((3, chunks, capacity, chunk), BF16),
            pltpu.VMEM((3, chunks, capacity, chunk), BF16),
            pltpu.VMEM((exp_dev, blocks, 8, capacity), F32),
            pltpu.VMEM((blocks, exp_dev, capacity, width), BF16),
            pltpu.VMEM((blocks, exp_dev, capacity, width), BF16),
            pltpu.VMEM((2, groups, exp_dev, peer, width), BF16),
            pltpu.VMEM((2, half_lanes, groups, peer, width), BF16),
            pltpu.VMEM((exp_dev, groups, peer, width), BF16),
            pltpu.VMEM((experts, peer, width), BF16),
            pltpu.VMEM((experts, tok_dev, peer), BF16),
            pltpu.VMEM((half_lanes, capacity, width), F32),
            dma((7,)),
            dma((3, chunks)), dma((3, chunks)),
            dma((lanes,)), dma((exp_dev, blocks)),
            dma((blocks, exp_dev)), dma((blocks, exp_dev)),
            dma((2, groups, exp_dev)), dma((2, half_lanes, groups)), dma((2, exp_dev, groups, blocks)),
            dma((exp_dev, groups)), dma((experts,)),
        ],
        compiler_params=pltpu.CompilerParams(
            collective_id=0, has_side_effects=True, vmem_limit_bytes=40 * 1024 * 1024
        ),
        name="layer",
    )(*operands)
    grad_tokens, grad_combine, grad_gate, grad_up, grad_down = pl.pallas_call(
        write_kernel,
        out_shape=results,
        in_specs=[anywhere] * 5,
        out_specs=[anywhere] * 5,
        scratch_shapes=[dma((5,))],
        compiler_params=pltpu.CompilerParams(vmem_limit_bytes=1024 * 1024),
        name="write_out",
    )(*[pltpu.with_memory_space_constraint(a, pltpu.VMEM) for a in held])
    return grad_tokens, grad_gate, grad_up, grad_down, grad_combine


def solution(mesh):
    placed = (
        P("expert", "mp"),
        P("expert", "mp"),
        P("expert", None, "mp"),
        P("expert", None, "mp"),
        P("expert", "mp", None),
        P("expert", None),
        P(),
    )
    return jax.shard_map(
        local,
        mesh=mesh,
        in_specs=placed,
        out_specs=(
            P("expert", "mp"),
            P("expert", None, "mp"),
            P("expert", None, "mp"),
            P("expert", "mp", None),
            P("expert", None),
        ),
        check_vma=False,
    )
```

```python
import functools

import jax
import jax.numpy as jnp
from jax import lax
from jax.experimental import pallas as pl
from jax.experimental.pallas import tpu as pltpu
from jax.sharding import PartitionSpec as P

MESH = pl.DeviceIdType.MESH
F32 = jnp.float32
BF16 = jnp.bfloat16


def nn(a, b):
    return jnp.dot(a, b, preferred_element_type=F32)


def nt(a, b):
    return lax.dot_general(a, b, (((1,), (1,)), ((), ())), preferred_element_type=F32)


def tn(a, b):
    return lax.dot_general(a, b, (((0,), (0,)), ((), ())), preferred_element_type=F32)


def layer_kernel(
    dims,
    x_hbm, cot_hbm, wg_hbm, wu_hbm, wd_hbm, combine_hbm, idx_hbm,
    tokens_ref, terms_ref, grad_gate, grad_up, grad_down,
    rows_in_ref, scaled_ref, act_ref, dgate_ref, dup_ref,
    x_ref, cot_ref, combine_ref, idx_ref, wg, wu, wd, rows_out, mine, ex_send, ex_recv,
    term_buf, red_send, red_recv, xs_send, xs_recv, bk_send, bk_recv, place, acc, rows_in_t,
    w_sem, x_send, x_recv,
    c_send, c_recv, r_send, r_recv, s_send, s_recv, sf_send, k_send, k_recv,
):
    (groups, lanes, exp_dev, blocks, half_lanes, tok_dev, width, capacity, hidden, chunk, peer) = dims
    half_width = half_lanes * width
    experts = groups * exp_dev
    chunks = hidden // chunk
    z = lax.axis_index("expert")
    lane = lax.axis_index("mp")
    own_b = lax.rem(lane, blocks)
    own_h = lax.rem(lax.div(lane, blocks), 2)
    own_e = lax.div(lane, 2 * blocks)
    feat_half = lax.div(lane, half_lanes)
    feat_pos = lax.rem(lane, half_lanes)

    def lane_of(e, h, b):
        return (e * 2 + h) * blocks + b

    def remote(src, dst, ssem, rsem, to_z, to_lane):
        return pltpu.make_async_remote_copy(
            src_ref=src, dst_ref=dst, send_sem=ssem, recv_sem=rsem,
            device_id=(to_z, to_lane), device_id_type=MESH,
        )

    def arrived(ref, ssem, rsem):
        remote(ref, ref, ssem, rsem, z, lane).wait_recv()

    loads = [
        pltpu.make_async_copy(src, dst, w_sem.at[i])
        for i, (src, dst) in enumerate((
            (idx_hbm, idx_ref), (x_hbm, x_ref), (combine_hbm, combine_ref), (cot_hbm, cot_ref),
            (wg_hbm.at[0], wg), (wu_hbm.at[0], wu), (wd_hbm.at[0], wd),
        ))
    ]
    for load in loads:
        load.start()

    barrier = pltpu.get_barrier_semaphore()
    for d in range(1, groups):
        for e in range(exp_dev):
            for other in (lane_of(e, feat_half, own_b), own_h * half_lanes + e * blocks + own_b):
                pl.semaphore_signal(barrier, inc=1, device_id=(lax.rem(z + d, groups), other), device_id_type=MESH)
    for d in range(1, lanes):
        pl.semaphore_signal(barrier, inc=1, device_id=(z, lax.rem(lane + d, lanes)), device_id_type=MESH)
    def iota(shape, axis):
        return lax.broadcasted_iota(jnp.int32, shape, axis)

    def before(row, g):
        return jnp.sum(jnp.where((row >= 0) & (row < g * tok_dev), 1.0, 0.0), axis=1, keepdims=True)

    def ones_where(condition):
        return jnp.where(condition, 1.0, 0.0).astype(BF16)

    def token_slot(row):
        return ones_where(iota((tok_dev, capacity), 0) + z * tok_dev == row)

    def row_slot(row, g):
        ahead = iota((peer, capacity), 1) - iota((peer, capacity), 0)
        return ones_where(ahead.astype(F32) == before(row, g))

    loads[0].wait()
    loads[1].wait()
    loads[3].wait()
    for d in range(groups):
        g = lax.rem(z + d, groups)
        for e in range(exp_dev):
            row = idx_ref[pl.ds(g * exp_dev + e, 1), :]
            pick = nt(row_slot(row, z), token_slot(row)).astype(BF16)
            xs_send[0, d, e] = nn(pick, x_ref[...]).astype(BF16)
            xs_send[1, d, e] = nn(pick, cot_ref[...]).astype(BF16)

    pl.semaphore_wait(barrier, lanes - 1 + (groups - 1) * 2 * exp_dev)

    sends = []

    def send_rows(kind, d, e):
        return remote(xs_send.at[kind, d, e], xs_recv.at[kind, feat_pos, z], s_send.at[kind, d, e],
                      s_recv.at[kind, feat_pos, z], lax.rem(z + d, groups), lane_of(e, feat_half, own_b))

    def start_rows(kind):
        for d in range(1, groups):
            for e in range(exp_dev):
                send_rows(kind, d, e).start()
        for e in range(exp_dev):
            target = lane_of(e, feat_half, own_b)

            @pl.when(target == lane)
            def _():
                xs_recv[kind, feat_pos, z] = xs_send[kind, 0, e]

            @pl.when(target != lane)
            def _():
                send_rows(kind, 0, e).start()

    def finish_rows(kind):
        for d in range(1, groups):
            for e in range(exp_dev):
                send_rows(kind, d, e).wait_send()
        for e in range(exp_dev):
            @pl.when(lane_of(e, feat_half, own_b) != lane)
            def _():
                send_rows(kind, 0, e).wait_send()

    start_rows(0)

    eye = iota((capacity, capacity), 0) == iota((capacity, capacity), 1)

    def column(row):
        return jnp.sum(jnp.where(eye, jnp.broadcast_to(row, (capacity, capacity)), 0.0), axis=1, keepdims=True)

    loads[2].wait()
    weight = column(combine_ref[pl.ds(own_e, 1), :])
    own_row = idx_ref[pl.ds(z * exp_dev + own_e, 1), :]

    def slot_map(axis):
        shape = (capacity, groups * peer) if axis else (groups * peer, capacity)
        spot, slot = iota(shape, axis), iota(shape, 1 - axis)
        total = jnp.zeros(shape, F32)
        for g in range(groups):
            hit = (slot - spot + g * peer).astype(F32) == before(own_row, g)
            total += jnp.where(hit & (spot >= g * peer) & (spot < (g + 1) * peer), 1.0, 0.0)
        return total.astype(BF16)

    to_slots = slot_map(1)

    def arrive_rows(kind, rows_ref):
        for d in range(groups):
            zs = lax.rem(z + d, groups)
            for j in range(exp_dev):
                p = j * blocks + own_b
                source = own_h * half_lanes + p

                @pl.when((source != lane) | (d > 0))
                def _():
                    arrived(xs_recv.at[kind, p, zs], s_send.at[kind, 0, 0], s_recv.at[kind, p, zs])

                for n in range(1, blocks):
                    copy = remote(xs_recv.at[kind, p, zs], xs_recv.at[kind, p, zs], sf_send.at[kind, j, zs, n],
                                  s_recv.at[kind, p, zs], z, lane_of(own_e, own_h, lax.rem(own_b + n, blocks)))
                    copy.start()
                    sends.append(copy)
        for d in range(groups):
            zs = lax.rem(z + d, groups)
            for n in range(1, blocks):
                for j in range(exp_dev):
                    p = j * blocks + lax.rem(own_b + n, blocks)
                    arrived(xs_recv.at[kind, p, zs], s_send.at[kind, 0, 0], s_recv.at[kind, p, zs])
        for p in range(half_lanes):
            packed = xs_recv[kind, p].reshape(groups * peer, width)
            rows_ref[:, p * width:(p + 1) * width] = nn(to_slots, packed).astype(BF16)

    finish_rows(0)
    start_rows(1)
    arrive_rows(0, rows_in_ref)

    partner = lane_of(own_e, 1 - own_h, own_b)

    def exchange_sum(which, c, value):
        cols = slice(c * chunk, (c + 1) * chunk)
        mine[which, :, cols] = value
        ex_send[which, c] = value.astype(BF16)
        copy = remote(ex_send.at[which, c], ex_recv.at[which, c], x_send.at[which, c],
                      x_recv.at[which, c], z, partner)
        copy.start()
        sends.append(copy)

    loads[4].wait()
    loads[5].wait()
    for c in range(chunks):
        cols = slice(c * chunk, (c + 1) * chunk)
        exchange_sum(0, c, nn(rows_in_ref[...], wg[:, cols]))
        exchange_sum(1, c, nn(rows_in_ref[...], wu[:, cols]))

    arrive_rows(1, rows_out)
    scaled_ref[...] = (weight * rows_out[...].astype(F32)).astype(BF16)
    loads[6].wait()
    for c in range(chunks):
        cols = slice(c * chunk, (c + 1) * chunk)
        exchange_sum(2, c, nt(rows_out[...], wd[cols, :]))

    from_slots = slot_map(0)
    for e in range(experts):
        row = idx_ref[e:e + 1, :]
        place[e] = nt(token_slot(row), row_slot(row, z)).astype(BF16)
    rows_in_t[...] = rows_in_ref[...].T

    def sum_arrived(which, c):
        arrived(ex_recv.at[which, c], x_send.at[which, c], x_recv.at[which, c])
        return mine[which, :, c * chunk:(c + 1) * chunk] + ex_recv[which, c].astype(F32)

    for c in range(chunks):
        cols = slice(c * chunk, (c + 1) * chunk)
        gate = sum_arrived(0, c)
        up = sum_arrived(1, c)
        s = jax.nn.sigmoid(gate)
        swish = gate * s
        act_ref[:, cols] = (swish * up).astype(BF16)
        mine[0, :, cols] = up * s * (1.0 + gate * (1.0 - s))
        mine[1, :, cols] = swish
        grad_down[0, cols, :] = tn(act_ref[:, cols], scaled_ref[...]).astype(BF16)

    def part_of(p, cols):
        rows = pl.ds(pl.multiple_of(p * width, width), width)
        return nt(dgate_ref[:, cols], wg[rows, cols]) + nt(dup_ref[:, cols], wu[rows, cols])

    slot_term = jnp.zeros((capacity, 1), F32)
    for c in range(chunks):
        cols = slice(c * chunk, (c + 1) * chunk)
        back = sum_arrived(2, c)
        slot_term += jnp.sum(act_ref[:, cols].astype(F32) * back, axis=1, keepdims=True)
        a = weight * back
        dgate_ref[:, cols] = (a * mine[0, :, cols]).astype(BF16)
        dup_ref[:, cols] = (a * mine[1, :, cols]).astype(BF16)
        if c < chunks - 1:
            for p in range(half_lanes):
                if c == 0:
                    acc[p] = part_of(p, cols)
                else:
                    acc[p] += part_of(p, cols)

    def block_part(p):
        last = part_of(p, slice((chunks - 1) * chunk, hidden))
        return acc[p] + last if chunks > 1 else last

    for d in range(1, blocks):
        to_b = lax.rem(own_b + d, blocks)
        for j in range(exp_dev):
            red_send[d, j] = block_part(j * blocks + to_b).astype(BF16)
            copy = remote(red_send.at[d, j], red_recv.at[own_b, j], r_send.at[d, j], r_recv.at[own_b, j],
                          z, lane_of(own_e, own_h, to_b))
            copy.start()
            sends.append(copy)
    def send_back(j, d):
        g = lax.rem(z + d, groups)
        slot = z * exp_dev + own_e
        return remote(bk_send.at[j, g], bk_recv.at[slot], k_send.at[j, d], k_recv.at[slot],
                      g, own_h * half_lanes + j * blocks + own_b)

    for j in range(exp_dev):
        total = block_part(j * blocks + own_b).astype(BF16).astype(F32)
        for d in range(1, blocks):
            from_b = lax.rem(own_b + d, blocks)
            arrived(red_recv.at[from_b, j], r_send.at[d, j], r_recv.at[from_b, j])
            total += red_recv[from_b, j].astype(F32)
        bk_send[j] = nn(from_slots, total.astype(BF16)).astype(BF16).reshape(groups, peer, width)
        for d in range(1, groups):
            copy = send_back(j, d)
            copy.start()
            sends.append(copy)
        target = own_h * half_lanes + j * blocks + own_b

        @pl.when(target == lane)
        def _():
            bk_recv[z * exp_dev + own_e] = bk_send[j, z]

        @pl.when(target != lane)
        def _():
            send_back(j, 0).start()

    term_row = jnp.sum(jnp.where(eye, jnp.broadcast_to(slot_term, (capacity, capacity)), 0.0), axis=0, keepdims=True)

    @pl.when(own_h == 0)
    def _():
        term_buf[own_e, own_b] = jnp.broadcast_to(term_row, (8, capacity))
        for d in range(1, lanes):
            remote(term_buf.at[own_e, own_b], term_buf.at[own_e, own_b], c_send.at[d],
                   c_recv.at[own_e, own_b], z, lax.rem(lane + d, lanes)).start()

    step = min(half_width, 256)
    for i in range(half_width // step):
        cols = slice(i * step, (i + 1) * step)
        grad_gate[0, cols, :] = nn(rows_in_t[cols, :], dgate_ref[...]).astype(BF16)
        grad_up[0, cols, :] = nn(rows_in_t[cols, :], dup_ref[...]).astype(BF16)
    for e in range(exp_dev):
        for b in range(blocks):
            @pl.when(lane_of(e, 0, b) != lane)
            def _():
                arrived(term_buf.at[e, b], c_send.at[1], c_recv.at[e, b])
        row = term_buf[e, 0, 0:1, :]
        for b in range(1, blocks):
            row += term_buf[e, b, 0:1, :]
        terms_ref[e:e + 1, :] = row

    total = jnp.zeros((tok_dev, width), F32)
    for d in range(groups):
        zs = lax.rem(z + d, groups)
        for e in range(exp_dev):
            slot = zs * exp_dev + e

            @pl.when((lane_of(e, feat_half, own_b) != lane) | (d > 0))
            def _():
                arrived(bk_recv.at[slot], k_send.at[0, 0], k_recv.at[slot])

            total += nn(place[slot], bk_recv[slot])
    tokens_ref[...] = total.astype(BF16)

    for copy in sends:
        copy.wait_send()
    finish_rows(1)
    for j in range(exp_dev):
        @pl.when(own_h * half_lanes + j * blocks + own_b != lane)
        def _():
            send_back(j, 0).wait_send()

    @pl.when(own_h == 0)
    def _():
        for d in range(1, lanes):
            remote(term_buf.at[own_e, own_b], term_buf.at[own_e, own_b], c_send.at[d],
                   c_recv.at[own_e, own_b], z, lax.rem(lane + d, lanes)).wait_send()


def write_kernel(*refs):
    count = len(refs) // 2
    copies = [
        pltpu.make_async_copy(src, dst, refs[-1].at[i])
        for i, (src, dst) in enumerate(zip(refs[:count], refs[count:2 * count]))
    ]
    for copy in copies:
        copy.start()
    for copy in copies:
        copy.wait()


def local(x_tokens, cotangent, w_gate, w_up, w_down, combine, indices):
    groups = lax.axis_size("expert")
    lanes = lax.axis_size("mp")
    tok_dev, width = x_tokens.shape
    experts, capacity = indices.shape
    exp_dev = experts // groups
    blocks = lanes // (2 * exp_dev)
    half_lanes = lanes // 2
    half_width, hidden = w_gate.shape[1:]
    chunk = min(hidden, 256)
    chunks = hidden // chunk
    peer = max(2 * capacity // groups, 16)
    dims = (groups, lanes, exp_dev, blocks, half_lanes, tok_dev, width, capacity, hidden, chunk, peer)
    vmem = pl.BlockSpec(memory_space=pltpu.VMEM)
    anywhere = pl.BlockSpec(memory_space=pl.ANY)
    dma = pltpu.SemaphoreType.DMA
    slot_half = jax.ShapeDtypeStruct((capacity, half_width), BF16)
    slot_hidden = jax.ShapeDtypeStruct((capacity, hidden), BF16)
    results = [
        jax.ShapeDtypeStruct((tok_dev, width), BF16),
        jax.ShapeDtypeStruct((exp_dev, capacity), F32),
        jax.ShapeDtypeStruct(w_gate.shape, BF16),
        jax.ShapeDtypeStruct(w_up.shape, BF16),
        jax.ShapeDtypeStruct(w_down.shape, BF16),
    ]
    operands = [
        pltpu.with_memory_space_constraint(a, pltpu.HBM)
        for a in (x_tokens, cotangent, w_gate, w_up, w_down, combine, indices)
    ]
    held = pl.pallas_call(
        functools.partial(layer_kernel, dims),
        out_shape=results,
        in_specs=[pl.BlockSpec(memory_space=pltpu.HBM)] * 7,
        out_specs=[vmem] * 5,
        scratch_shapes=[
            pltpu.VMEM((capacity, half_width), BF16),
            pltpu.VMEM((capacity, half_width), BF16),
            pltpu.VMEM((capacity, hidden), BF16),
            pltpu.VMEM((capacity, hidden), BF16),
            pltpu.VMEM((capacity, hidden), BF16),
            pltpu.VMEM((tok_dev, width), BF16),
            pltpu.VMEM((tok_dev, width), BF16),
            pltpu.VMEM((exp_dev, capacity), F32),
            pltpu.VMEM((experts, capacity), jnp.int32),
            pltpu.VMEM((half_width, hidden), BF16),
            pltpu.VMEM((half_width, hidden), BF16),
            pltpu.VMEM((hidden, half_width), BF16),
            pltpu.VMEM((capacity, half_width), BF16),
            pltpu.VMEM((3, capacity, hidden), F32),
            pltpu.VMEM((3, chunks, capacity, chunk), BF16),
            pltpu.VMEM((3, chunks, capacity, chunk), BF16),
            pltpu.VMEM((exp_dev, blocks, 8, capacity), F32),
            pltpu.VMEM((blocks, exp_dev, capacity, width), BF16),
            pltpu.VMEM((blocks, exp_dev, capacity, width), BF16),
            pltpu.VMEM((2, groups, exp_dev, peer, width), BF16),
            pltpu.VMEM((2, half_lanes, groups, peer, width), BF16),
            pltpu.VMEM((exp_dev, groups, peer, width), BF16),
            pltpu.VMEM((experts, peer, width), BF16),
            pltpu.VMEM((experts, tok_dev, peer), BF16),
            pltpu.VMEM((half_lanes, capacity, width), F32),
            pltpu.VMEM((half_width, capacity), BF16),
            dma((7,)),
            dma((3, chunks)), dma((3, chunks)),
            dma((lanes,)), dma((exp_dev, blocks)),
            dma((blocks, exp_dev)), dma((blocks, exp_dev)),
            dma((2, groups, exp_dev)), dma((2, half_lanes, groups)), dma((2, exp_dev, groups, blocks)),
            dma((exp_dev, groups)), dma((experts,)),
        ],
        compiler_params=pltpu.CompilerParams(
            collective_id=0, has_side_effects=True, vmem_limit_bytes=40 * 1024 * 1024
        ),
        name="layer",
    )(*operands)
    grad_tokens, grad_combine, grad_gate, grad_up, grad_down = pl.pallas_call(
        write_kernel,
        out_shape=results,
        in_specs=[anywhere] * 5,
        out_specs=[anywhere] * 5,
        scratch_shapes=[dma((5,))],
        compiler_params=pltpu.CompilerParams(vmem_limit_bytes=1024 * 1024),
        name="write_out",
    )(*[pltpu.with_memory_space_constraint(a, pltpu.VMEM) for a in held])
    return grad_tokens, grad_gate, grad_up, grad_down, grad_combine


def solution(mesh):
    placed = (
        P("expert", "mp"),
        P("expert", "mp"),
        P("expert", None, "mp"),
        P("expert", None, "mp"),
        P("expert", "mp", None),
        P("expert", None),
        P(),
    )
    return jax.shard_map(
        local,
        mesh=mesh,
        in_specs=placed,
        out_specs=(
            P("expert", "mp"),
            P("expert", None, "mp"),
            P("expert", None, "mp"),
            P("expert", "mp", None),
            P("expert", None),
        ),
        check_vma=False,
    )
```

```python
import functools

import jax
import jax.numpy as jnp
from jax import lax
from jax.experimental import pallas as pl
from jax.experimental.pallas import tpu as pltpu
from jax.sharding import PartitionSpec as P

MESH = pl.DeviceIdType.MESH
F32 = jnp.float32
BF16 = jnp.bfloat16


def nn(a, b):
    return jnp.dot(a, b, preferred_element_type=F32)


def nt(a, b):
    return lax.dot_general(a, b, (((1,), (1,)), ((), ())), preferred_element_type=F32)


def tn(a, b):
    return lax.dot_general(a, b, (((0,), (0,)), ((), ())), preferred_element_type=F32)


def layer_kernel(
    dims,
    x_hbm, cot_hbm, wg_hbm, wu_hbm, wd_hbm, combine_hbm, idx_hbm,
    tokens_ref, terms_ref, grad_gate, grad_up, grad_down,
    rows_in_ref, scaled_ref, act_ref, dgate_ref, dup_ref,
    x_ref, cot_ref, combine_ref, idx_ref, wg, wu, wd, rows_out, mine, ex_send, ex_recv,
    term_buf, red_send, red_recv, xs_send, xs_recv, bk_send, bk_recv, place, acc, rows_in_t, picks,
    w_sem, x_send, x_recv,
    c_send, c_recv, r_send, r_recv, s_send, s_recv, sf_send, k_send, k_recv,
):
    (groups, lanes, exp_dev, blocks, half_lanes, tok_dev, width, capacity, hidden, chunk, peer) = dims
    half_width = half_lanes * width
    experts = groups * exp_dev
    chunks = hidden // chunk
    z = lax.axis_index("expert")
    lane = lax.axis_index("mp")
    own_b = lax.rem(lane, blocks)
    own_h = lax.rem(lax.div(lane, blocks), 2)
    own_e = lax.div(lane, 2 * blocks)
    feat_half = lax.div(lane, half_lanes)
    feat_pos = lax.rem(lane, half_lanes)

    def lane_of(e, h, b):
        return (e * 2 + h) * blocks + b

    def remote(src, dst, ssem, rsem, to_z, to_lane):
        return pltpu.make_async_remote_copy(
            src_ref=src, dst_ref=dst, send_sem=ssem, recv_sem=rsem,
            device_id=(to_z, to_lane), device_id_type=MESH,
        )

    def arrived(ref, ssem, rsem):
        remote(ref, ref, ssem, rsem, z, lane).wait_recv()

    loads = [
        pltpu.make_async_copy(src, dst, w_sem.at[i])
        for i, (src, dst) in enumerate((
            (idx_hbm, idx_ref), (x_hbm, x_ref), (combine_hbm, combine_ref), (cot_hbm, cot_ref),
            (wg_hbm.at[0], wg), (wu_hbm.at[0], wu), (wd_hbm.at[0], wd),
        ))
    ]
    for load in loads:
        load.start()

    barrier = pltpu.get_barrier_semaphore()
    for d in range(1, groups):
        for e in range(exp_dev):
            for other in (lane_of(e, feat_half, own_b), own_h * half_lanes + e * blocks + own_b):
                pl.semaphore_signal(barrier, inc=1, device_id=(lax.rem(z + d, groups), other), device_id_type=MESH)
    for d in range(1, lanes):
        pl.semaphore_signal(barrier, inc=1, device_id=(z, lax.rem(lane + d, lanes)), device_id_type=MESH)
    def iota(shape, axis):
        return lax.broadcasted_iota(jnp.int32, shape, axis)

    def before(row, g):
        return jnp.sum(jnp.where((row >= 0) & (row < g * tok_dev), 1.0, 0.0), axis=1, keepdims=True)

    def ones_where(condition):
        return jnp.where(condition, 1.0, 0.0).astype(BF16)

    def token_slot(row):
        return ones_where(iota((tok_dev, capacity), 0) + z * tok_dev == row)

    def row_slot(row, g):
        ahead = iota((peer, capacity), 1) - iota((peer, capacity), 0)
        return ones_where(ahead.astype(F32) == before(row, g))

    loads[0].wait()
    loads[1].wait()
    for d in range(groups):
        g = lax.rem(z + d, groups)
        for e in range(exp_dev):
            row = idx_ref[pl.ds(g * exp_dev + e, 1), :]
            picks[d, e] = nt(row_slot(row, z), token_slot(row)).astype(BF16)
            xs_send[0, d, e] = nn(picks[d, e], x_ref[...]).astype(BF16)

    pl.semaphore_wait(barrier, lanes - 1 + (groups - 1) * 2 * exp_dev)

    sends = []

    def send_rows(kind, d, e):
        return remote(xs_send.at[kind, d, e], xs_recv.at[kind, feat_pos, z], s_send.at[kind, d, e],
                      s_recv.at[kind, feat_pos, z], lax.rem(z + d, groups), lane_of(e, feat_half, own_b))

    def start_rows(kind):
        for d in range(1, groups):
            for e in range(exp_dev):
                send_rows(kind, d, e).start()
        for e in range(exp_dev):
            target = lane_of(e, feat_half, own_b)

            @pl.when(target == lane)
            def _():
                xs_recv[kind, feat_pos, z] = xs_send[kind, 0, e]

            @pl.when(target != lane)
            def _():
                send_rows(kind, 0, e).start()

    def finish_rows(kind):
        for d in range(1, groups):
            for e in range(exp_dev):
                send_rows(kind, d, e).wait_send()
        for e in range(exp_dev):
            @pl.when(lane_of(e, feat_half, own_b) != lane)
            def _():
                send_rows(kind, 0, e).wait_send()

    start_rows(0)
    loads[3].wait()
    for d in range(groups):
        for e in range(exp_dev):
            xs_send[1, d, e] = nn(picks[d, e], cot_ref[...]).astype(BF16)

    eye = iota((capacity, capacity), 0) == iota((capacity, capacity), 1)

    def column(row):
        return jnp.sum(jnp.where(eye, jnp.broadcast_to(row, (capacity, capacity)), 0.0), axis=1, keepdims=True)

    loads[2].wait()
    weight = column(combine_ref[pl.ds(own_e, 1), :])
    own_row = idx_ref[pl.ds(z * exp_dev + own_e, 1), :]

    def slot_map(axis):
        shape = (capacity, groups * peer) if axis else (groups * peer, capacity)
        spot, slot = iota(shape, axis), iota(shape, 1 - axis)
        total = jnp.zeros(shape, F32)
        for g in range(groups):
            hit = (slot - spot + g * peer).astype(F32) == before(own_row, g)
            total += jnp.where(hit & (spot >= g * peer) & (spot < (g + 1) * peer), 1.0, 0.0)
        return total.astype(BF16)

    to_slots = slot_map(1)

    def arrive_rows(kind, rows_ref):
        for d in range(groups):
            zs = lax.rem(z + d, groups)
            for j in range(exp_dev):
                p = j * blocks + own_b
                source = own_h * half_lanes + p

                @pl.when((source != lane) | (d > 0))
                def _():
                    arrived(xs_recv.at[kind, p, zs], s_send.at[kind, 0, 0], s_recv.at[kind, p, zs])

                for n in range(1, blocks):
                    copy = remote(xs_recv.at[kind, p, zs], xs_recv.at[kind, p, zs], sf_send.at[kind, j, zs, n],
                                  s_recv.at[kind, p, zs], z, lane_of(own_e, own_h, lax.rem(own_b + n, blocks)))
                    copy.start()
                    sends.append(copy)
        for d in range(groups):
            zs = lax.rem(z + d, groups)
            for n in range(1, blocks):
                for j in range(exp_dev):
                    p = j * blocks + lax.rem(own_b + n, blocks)
                    arrived(xs_recv.at[kind, p, zs], s_send.at[kind, 0, 0], s_recv.at[kind, p, zs])
        for p in range(half_lanes):
            packed = xs_recv[kind, p].reshape(groups * peer, width)
            rows_ref[:, p * width:(p + 1) * width] = nn(to_slots, packed).astype(BF16)

    finish_rows(0)
    start_rows(1)
    arrive_rows(0, rows_in_ref)

    partner = lane_of(own_e, 1 - own_h, own_b)

    def exchange_sum(which, c, value):
        cols = slice(c * chunk, (c + 1) * chunk)
        mine[which, :, cols] = value
        ex_send[which, c] = value.astype(BF16)
        copy = remote(ex_send.at[which, c], ex_recv.at[which, c], x_send.at[which, c],
                      x_recv.at[which, c], z, partner)
        copy.start()
        sends.append(copy)

    loads[4].wait()
    loads[5].wait()
    for c in range(chunks):
        cols = slice(c * chunk, (c + 1) * chunk)
        exchange_sum(0, c, nn(rows_in_ref[...], wg[:, cols]))
        exchange_sum(1, c, nn(rows_in_ref[...], wu[:, cols]))

    arrive_rows(1, rows_out)
    scaled_ref[...] = (weight * rows_out[...].astype(F32)).astype(BF16)
    loads[6].wait()
    for c in range(chunks):
        cols = slice(c * chunk, (c + 1) * chunk)
        exchange_sum(2, c, nt(rows_out[...], wd[cols, :]))

    from_slots = slot_map(0)
    for e in range(experts):
        row = idx_ref[e:e + 1, :]
        place[e] = nt(token_slot(row), row_slot(row, z)).astype(BF16)
    rows_in_t[...] = rows_in_ref[...].T

    def sum_arrived(which, c):
        arrived(ex_recv.at[which, c], x_send.at[which, c], x_recv.at[which, c])
        return mine[which, :, c * chunk:(c + 1) * chunk] + ex_recv[which, c].astype(F32)

    for c in range(chunks):
        cols = slice(c * chunk, (c + 1) * chunk)
        gate = sum_arrived(0, c)
        up = sum_arrived(1, c)
        s = jax.nn.sigmoid(gate)
        swish = gate * s
        act_ref[:, cols] = (swish * up).astype(BF16)
        mine[0, :, cols] = up * s * (1.0 + gate * (1.0 - s))
        mine[1, :, cols] = swish
        grad_down[0, cols, :] = tn(act_ref[:, cols], scaled_ref[...]).astype(BF16)

    def part_of(p, cols):
        rows = pl.ds(pl.multiple_of(p * width, width), width)
        return nt(dgate_ref[:, cols], wg[rows, cols]) + nt(dup_ref[:, cols], wu[rows, cols])

    slot_term = jnp.zeros((capacity, 1), F32)
    for c in range(chunks):
        cols = slice(c * chunk, (c + 1) * chunk)
        back = sum_arrived(2, c)
        slot_term += jnp.sum(act_ref[:, cols].astype(F32) * back, axis=1, keepdims=True)
        a = weight * back
        dgate_ref[:, cols] = (a * mine[0, :, cols]).astype(BF16)
        dup_ref[:, cols] = (a * mine[1, :, cols]).astype(BF16)
        if c < chunks - 1:
            for p in range(half_lanes):
                if c == 0:
                    acc[p] = part_of(p, cols)
                else:
                    acc[p] += part_of(p, cols)

    def block_part(p):
        last = part_of(p, slice((chunks - 1) * chunk, hidden))
        return acc[p] + last if chunks > 1 else last

    for d in range(1, blocks):
        to_b = lax.rem(own_b + d, blocks)
        for j in range(exp_dev):
            red_send[d, j] = block_part(j * blocks + to_b).astype(BF16)
            copy = remote(red_send.at[d, j], red_recv.at[own_b, j], r_send.at[d, j], r_recv.at[own_b, j],
                          z, lane_of(own_e, own_h, to_b))
            copy.start()
            sends.append(copy)
    def send_back(j, d):
        g = lax.rem(z + d, groups)
        slot = z * exp_dev + own_e
        return remote(bk_send.at[j, g], bk_recv.at[slot], k_send.at[j, d], k_recv.at[slot],
                      g, own_h * half_lanes + j * blocks + own_b)

    for j in range(exp_dev):
        total = block_part(j * blocks + own_b).astype(BF16).astype(F32)
        for d in range(1, blocks):
            from_b = lax.rem(own_b + d, blocks)
            arrived(red_recv.at[from_b, j], r_send.at[d, j], r_recv.at[from_b, j])
            total += red_recv[from_b, j].astype(F32)
        bk_send[j] = nn(from_slots, total.astype(BF16)).astype(BF16).reshape(groups, peer, width)
        for d in range(1, groups):
            copy = send_back(j, d)
            copy.start()
            sends.append(copy)
        target = own_h * half_lanes + j * blocks + own_b

        @pl.when(target == lane)
        def _():
            bk_recv[z * exp_dev + own_e] = bk_send[j, z]

        @pl.when(target != lane)
        def _():
            send_back(j, 0).start()

    term_row = jnp.sum(jnp.where(eye, jnp.broadcast_to(slot_term, (capacity, capacity)), 0.0), axis=0, keepdims=True)

    @pl.when(own_h == 0)
    def _():
        term_buf[own_e, own_b] = jnp.broadcast_to(term_row, (8, capacity))
        for d in range(1, lanes):
            remote(term_buf.at[own_e, own_b], term_buf.at[own_e, own_b], c_send.at[d],
                   c_recv.at[own_e, own_b], z, lax.rem(lane + d, lanes)).start()

    step = min(half_width, 256)
    for i in range(half_width // step):
        cols = slice(i * step, (i + 1) * step)
        grad_gate[0, cols, :] = nn(rows_in_t[cols, :], dgate_ref[...]).astype(BF16)
        grad_up[0, cols, :] = nn(rows_in_t[cols, :], dup_ref[...]).astype(BF16)
    for e in range(exp_dev):
        for b in range(blocks):
            @pl.when(lane_of(e, 0, b) != lane)
            def _():
                arrived(term_buf.at[e, b], c_send.at[1], c_recv.at[e, b])
        row = term_buf[e, 0, 0:1, :]
        for b in range(1, blocks):
            row += term_buf[e, b, 0:1, :]
        terms_ref[e:e + 1, :] = row

    total = jnp.zeros((tok_dev, width), F32)
    for d in range(groups):
        zs = lax.rem(z + d, groups)
        for e in range(exp_dev):
            slot = zs * exp_dev + e

            @pl.when((lane_of(e, feat_half, own_b) != lane) | (d > 0))
            def _():
                arrived(bk_recv.at[slot], k_send.at[0, 0], k_recv.at[slot])

            total += nn(place[slot], bk_recv[slot])
    tokens_ref[...] = total.astype(BF16)

    for copy in sends:
        copy.wait_send()
    finish_rows(1)
    for j in range(exp_dev):
        @pl.when(own_h * half_lanes + j * blocks + own_b != lane)
        def _():
            send_back(j, 0).wait_send()

    @pl.when(own_h == 0)
    def _():
        for d in range(1, lanes):
            remote(term_buf.at[own_e, own_b], term_buf.at[own_e, own_b], c_send.at[d],
                   c_recv.at[own_e, own_b], z, lax.rem(lane + d, lanes)).wait_send()


def write_kernel(*refs):
    count = len(refs) // 2
    copies = [
        pltpu.make_async_copy(src, dst, refs[-1].at[i])
        for i, (src, dst) in enumerate(zip(refs[:count], refs[count:2 * count]))
    ]
    for copy in copies:
        copy.start()
    for copy in copies:
        copy.wait()


def local(x_tokens, cotangent, w_gate, w_up, w_down, combine, indices):
    groups = lax.axis_size("expert")
    lanes = lax.axis_size("mp")
    tok_dev, width = x_tokens.shape
    experts, capacity = indices.shape
    exp_dev = experts // groups
    blocks = lanes // (2 * exp_dev)
    half_lanes = lanes // 2
    half_width, hidden = w_gate.shape[1:]
    chunk = min(hidden, 256)
    chunks = hidden // chunk
    peer = max(2 * capacity // groups, 16)
    dims = (groups, lanes, exp_dev, blocks, half_lanes, tok_dev, width, capacity, hidden, chunk, peer)
    vmem = pl.BlockSpec(memory_space=pltpu.VMEM)
    anywhere = pl.BlockSpec(memory_space=pl.ANY)
    dma = pltpu.SemaphoreType.DMA
    slot_half = jax.ShapeDtypeStruct((capacity, half_width), BF16)
    slot_hidden = jax.ShapeDtypeStruct((capacity, hidden), BF16)
    results = [
        jax.ShapeDtypeStruct((tok_dev, width), BF16),
        jax.ShapeDtypeStruct((exp_dev, capacity), F32),
        jax.ShapeDtypeStruct(w_gate.shape, BF16),
        jax.ShapeDtypeStruct(w_up.shape, BF16),
        jax.ShapeDtypeStruct(w_down.shape, BF16),
    ]
    operands = [
        pltpu.with_memory_space_constraint(a, pltpu.HBM)
        for a in (x_tokens, cotangent, w_gate, w_up, w_down, combine, indices)
    ]
    held = pl.pallas_call(
        functools.partial(layer_kernel, dims),
        out_shape=results,
        in_specs=[pl.BlockSpec(memory_space=pltpu.HBM)] * 7,
        out_specs=[vmem] * 5,
        scratch_shapes=[
            pltpu.VMEM((capacity, half_width), BF16),
            pltpu.VMEM((capacity, half_width), BF16),
            pltpu.VMEM((capacity, hidden), BF16),
            pltpu.VMEM((capacity, hidden), BF16),
            pltpu.VMEM((capacity, hidden), BF16),
            pltpu.VMEM((tok_dev, width), BF16),
            pltpu.VMEM((tok_dev, width), BF16),
            pltpu.VMEM((exp_dev, capacity), F32),
            pltpu.VMEM((experts, capacity), jnp.int32),
            pltpu.VMEM((half_width, hidden), BF16),
            pltpu.VMEM((half_width, hidden), BF16),
            pltpu.VMEM((hidden, half_width), BF16),
            pltpu.VMEM((capacity, half_width), BF16),
            pltpu.VMEM((3, capacity, hidden), F32),
            pltpu.VMEM((3, chunks, capacity, chunk), BF16),
            pltpu.VMEM((3, chunks, capacity, chunk), BF16),
            pltpu.VMEM((exp_dev, blocks, 8, capacity), F32),
            pltpu.VMEM((blocks, exp_dev, capacity, width), BF16),
            pltpu.VMEM((blocks, exp_dev, capacity, width), BF16),
            pltpu.VMEM((2, groups, exp_dev, peer, width), BF16),
            pltpu.VMEM((2, half_lanes, groups, peer, width), BF16),
            pltpu.VMEM((exp_dev, groups, peer, width), BF16),
            pltpu.VMEM((experts, peer, width), BF16),
            pltpu.VMEM((experts, tok_dev, peer), BF16),
            pltpu.VMEM((half_lanes, capacity, width), F32),
            pltpu.VMEM((half_width, capacity), BF16),
            pltpu.VMEM((groups, exp_dev, peer, tok_dev), BF16),
            dma((7,)),
            dma((3, chunks)), dma((3, chunks)),
            dma((lanes,)), dma((exp_dev, blocks)),
            dma((blocks, exp_dev)), dma((blocks, exp_dev)),
            dma((2, groups, exp_dev)), dma((2, half_lanes, groups)), dma((2, exp_dev, groups, blocks)),
            dma((exp_dev, groups)), dma((experts,)),
        ],
        compiler_params=pltpu.CompilerParams(
            collective_id=0, has_side_effects=True, vmem_limit_bytes=40 * 1024 * 1024
        ),
        name="layer",
    )(*operands)
    grad_tokens, grad_combine, grad_gate, grad_up, grad_down = pl.pallas_call(
        write_kernel,
        out_shape=results,
        in_specs=[anywhere] * 5,
        out_specs=[anywhere] * 5,
        scratch_shapes=[dma((5,))],
        compiler_params=pltpu.CompilerParams(vmem_limit_bytes=1024 * 1024),
        name="write_out",
    )(*[pltpu.with_memory_space_constraint(a, pltpu.VMEM) for a in held])
    return grad_tokens, grad_gate, grad_up, grad_down, grad_combine


def solution(mesh):
    placed = (
        P("expert", "mp"),
        P("expert", "mp"),
        P("expert", None, "mp"),
        P("expert", None, "mp"),
        P("expert", "mp", None),
        P("expert", None),
        P(),
    )
    return jax.shard_map(
        local,
        mesh=mesh,
        in_specs=placed,
        out_specs=(
            P("expert", "mp"),
            P("expert", None, "mp"),
            P("expert", None, "mp"),
            P("expert", "mp", None),
            P("expert", None),
        ),
        check_vma=False,
    )
```
